1024 devices in a mesh: expert: 64 (over x, y, core), dp: 16 (over z).
Axes of the slice: x: 4, y: 8, z: 16, core: 2. Of those that a mesh axis runs over, the one named last changes fastest.
Arguments:
- x_t: bfloat16 [4096, 16384], P('expert', 'dp'), may hold values from -16 to 16
- down_proj: bfloat16 [4096, 1024], P('expert'), may hold values from -0.09375 to 0.09375
- w_gate: bfloat16 [64, 1024, 1024], P('expert'), may hold values from -0.1875 to 0.1875
- w_value: bfloat16 [64, 1024, 1024], P('expert'), may hold values from -0.1875 to 0.1875
- w_out: bfloat16 [64, 1024, 1024], P('expert'), may hold values from -0.1875 to 0.1875
- routes: int32 [16384, 4], P(('dp', 'expert')), may hold values from 0 to 63, all different within a row; in each aligned block of 16 rows (0 to 15, 16 to 31, ...) at most 2 rows name the same one
- gate_fix: int32 [16384, 4], P(('dp', 'expert')), may hold values from 6554 to 65535
- cotangent: bfloat16 [16384, 1024], P(('dp', 'expert')), may hold values from -6 to 6
Outputs:
- combined: bfloat16 [16384, 1024], P(('dp', 'expert'))
- grad_x: bfloat16 [4096, 16384], P('expert', 'dp')
- grad_down: float32 [4096, 1024], P('expert')
The draws below stay inside these ranges and needn't reach their ends.
Inputs may be any that keep to these rules, and one draw needn't show every extreme that they name: `routes`: each row names 4 different experts. Among the 16 rows of one device (aligned blocks of 16 rows) no expert is named by more than 2 rows, a bound that some block reaches. `gate_fix`: A gate weight is this integer divided by 65536.
All inputs are finite; a program needn't handle non-finite values.
Results may differ from the reference program's by a relative error of at most 0.023.
Values may be sent and summed in bfloat16 or wider, within the bound.
No kernel may reach another device: no remote copies, remote signals or barrier semaphores. Data moves between devices by JAX's collectives and lax.ppermute only.
A program may use at most 32 MiB of HBM per device.

```python
import math
import jax
import jax.numpy as jnp
import numpy as np
from jax import lax

D = 4096
L = 1024
H = 1024
TOP = 4
TOK_DEV = 16
EXPERTS = 64
CAP = 2
TOKENS = 16384
N_EXPERT = 64
N_DP = 16


def touch_ends(result, key, low, high):
    extent = result.shape
    index_at = [jax.random.randint(jax.random.fold_in(key, axis), (), 0, extent[axis]) for axis in range(len(extent))]
    result = result.at[tuple(index_at)].set(low)
    longest = extent.index(max(extent))
    index_at[longest] = (index_at[longest] + 1) % extent[longest]
    return result.at[tuple(index_at)].set(high)


def strengthened(entries, stream_key, source, target, parts, factor):
    def block_of(axis_at):
        return (jnp.arange(entries.shape[axis_at]) // (entries.shape[axis_at] // parts)).reshape((-1,) + (1,) * (entries.ndim - 1 - axis_at))

    one_side = jax.random.permutation(stream_key, parts)[block_of(target)]
    other_side = (block_of(target) + parts // 2) % parts
    return jnp.where((block_of(source) == one_side) | (block_of(source) == other_side), factor * entries, entries)


def shard_levels(rng, dims, shards, least, largest):
    def one(dim, shards_of):
        heights = jax.random.uniform(jax.random.fold_in(jax.random.fold_in(rng, 6), dim), (shards_of,), jnp.float32, least / len(shards), largest / len(shards))
        return jnp.repeat(jnp.exp(heights), dims[dim] // shards_of).reshape((-1,) + (1,) * (len(dims) - dim - 1))

    loudness = one(*shards[0])
    for cut in shards[1:]:
        loudness = loudness * one(*cut)
    return loudness


def assign_block(rng, own, number, rows, count, top, bound, skew):
    order = jax.random.permutation(rng, count)
    crowded, common = load_shares(count, rows * top, bound, skew, True), load_shares(count, rows * top, bound, skew, False)
    places = jnp.arange(count)

    def named(lengths, offset_by):
        used = int((lengths > 0).sum())
        fixed = max(1, used // 4)
        shifted = fixed + (places - fixed + offset_by * (used - fixed)) % max(1, count - fixed)
        return jnp.zeros((count,), jnp.int32).at[order[jnp.where(places < fixed, places, shifted)]].set(jnp.asarray(lengths, jnp.int32))

    lengths = jnp.where(number % 4 == 0, named(crowded, number // 4), named(common, number - number // 4 - 1))
    mixed = jax.random.permutation(jax.random.fold_in(own, 3), count)
    source_of, sink = mixed[0:count // 2 * 2:2], mixed[1:count // 2 * 2:2]
    room = jnp.minimum(lengths[source_of] - 1, bound - lengths[sink]) // 2
    room = jnp.where((source_of == order[0]) | (sink == order[0]) | (lengths[sink] == 0), 0, jnp.maximum(room, 0))
    shifted = jax.random.randint(jax.random.fold_in(own, 4), (count // 2,), 0, 1 << 20) % (room + 1)
    lengths = lengths.at[source_of].add(-shifted).at[sink].add(shifted)
    items = jnp.searchsorted(jnp.cumsum(lengths), jnp.arange(rows * top), side="right").astype(jnp.int32)
    listing = items.reshape(top, rows).T
    listing = listing[jax.random.permutation(jax.random.fold_in(own, 1), rows)]
    offset_by = jax.random.randint(jax.random.fold_in(own, 2), (rows, 1), 0, top)
    return jnp.take_along_axis(listing, (jnp.arange(top)[None, :] + offset_by) % top, axis=1)


def load_shares(amount, total, most, slope, full):
    loads = [(1 << 20) // math.isqrt(standing ** slope) + 1 for standing in range(1, amount + 1)]
    largest = most if full else min(most, max(-(-total // amount), total * loads[0] // sum(loads)))
    least = 1 if total - largest >= amount - 1 else 0
    given, rest = [largest] + [least] * (amount - 1), total - largest - least * (amount - 1)
    while rest > 0:
        free = [i for i in range(1, amount) if given[i] < largest] or [i for i in range(1, amount) if given[i] < most]
        pool, left = sum([loads[i] for i in free]), rest
        for i in free:
            more = min(most - given[i], max(1, left * loads[i] // pool), rest)
            given[i] = given[i] + more
            rest = rest - more
    return np.array(given)


def centred(rng, extent, width, bound, shards=(), kind=jnp.bfloat16):
    result = jax.random.normal(rng, extent, jnp.float32) * width
    if len(shards) > 0:
        result = shard_levels(rng, extent, shards, -0.22, 0.18) * result
    return jnp.clip(result, min=-bound, max=bound).astype(kind)


def bell_draw_with(own_key, shape, scale, bound, split, heavy, held_as=jnp.bfloat16):
    entries = scale * jax.random.normal(own_key, shape, jnp.float32)
    if split:
        entries = entries * shard_levels(own_key, shape, split, -0.22, 0.18)
    return jnp.clip(strengthened(entries, jax.random.fold_in(own_key, 3), *heavy), -bound, bound).astype(held_as)


def setup_inputs(seed: int = 0) -> dict:
    key_of = jax.random.split(jax.random.key(seed), 9)
    x_t = bell_draw_with(key_of[0], (D, TOKENS), 1.0, 16.0, ((0, 64), (1, 16)), (0, 1, 64, 4.0))
    down_proj = centred(key_of[1], (D, L), D ** -0.5, 0.09375, ((0, 64),))
    w_gate = centred(key_of[2], (EXPERTS, L, H), L ** -0.5, 0.1875, ((0, 64),))
    w_value = centred(key_of[3], (EXPERTS, L, H), L ** -0.5, 0.1875, ((0, 64),))
    w_out = centred(key_of[4], (EXPERTS, H, L), H ** -0.5, 0.1875, ((0, 64),))
    routes_keys = jax.random.split(jax.random.fold_in(key_of[5], 1), TOKENS // TOK_DEV)
    routes_turns = jax.random.permutation(jax.random.fold_in(key_of[5], 3), TOKENS // TOK_DEV)
    routes = jax.vmap(lambda own, number: assign_block(jax.random.fold_in(key_of[5], 2), own, number, TOK_DEV, EXPERTS, TOP, CAP, 2))(routes_keys, routes_turns).reshape((TOKENS, TOP))
    gate_fix = touch_ends(jax.random.randint(key_of[6], (TOKENS, TOP), 6554, 65536), jax.random.fold_in(key_of[6], 1), 6554, 65535).astype(jnp.int32)
    cotangent = centred(key_of[7], (TOKENS, L), 1.0, 6.0, ((0, 1024),))
    return dict(x_t=x_t, down_proj=down_proj, w_gate=w_gate, w_value=w_value, w_out=w_out, routes=routes, gate_fix=gate_fix, cotangent=cotangent)


fixed_unit = 65536.0

def reference(x_t, down_proj, w_gate, w_value, w_out, routes, gate_fix, cotangent):
    latent = jnp.dot(x_t.T, down_proj, preferred_element_type=jnp.float32).astype(jnp.bfloat16)
    gate_values = gate_fix.astype(jnp.float32) / fixed_unit
    grad_rows = (gate_values[:, :, None] * cotangent.astype(jnp.float32)[:, None, :]).astype(jnp.bfloat16)
    grad_rows = grad_rows.reshape(TOKENS * TOP, L)
    flat_routes = routes.reshape(-1)
    row_limit = N_DP * N_EXPERT * CAP

    def per_expert(expert, totals):
        out_total, grad_total = totals
        hits = flat_routes == expert
        positions = jnp.nonzero(hits, size=row_limit, fill_value=0)[0].astype(jnp.int32)
        in_use = (jnp.arange(row_limit) < jnp.sum(hits.astype(jnp.int32))).astype(jnp.float32)[:, None]
        chosen_rows = latent[positions // TOP]
        chosen_grads = grad_rows[positions]
        gate_matrix = lax.dynamic_index_in_dim(w_gate, expert, 0, keepdims=False)
        value_matrix = lax.dynamic_index_in_dim(w_value, expert, 0, keepdims=False)
        out_matrix = lax.dynamic_index_in_dim(w_out, expert, 0, keepdims=False)
        pre_gate = jnp.dot(chosen_rows, gate_matrix, preferred_element_type=jnp.float32)
        pre_value = jnp.dot(chosen_rows, value_matrix, preferred_element_type=jnp.float32)
        sigmoid_gate = jax.nn.sigmoid(pre_gate)
        activated = pre_gate * sigmoid_gate
        hidden = (activated * pre_value).astype(jnp.bfloat16)
        expert_out = jnp.dot(hidden, out_matrix, preferred_element_type=jnp.float32).astype(jnp.bfloat16)
        hidden_grad = jnp.dot(chosen_grads, out_matrix.T, preferred_element_type=jnp.float32)
        gate_grad = (hidden_grad * pre_value * sigmoid_gate * (1.0 + pre_gate * (1.0 - sigmoid_gate))).astype(jnp.bfloat16)
        value_grad = (hidden_grad * activated).astype(jnp.bfloat16)
        row_grad = (jnp.dot(gate_grad, gate_matrix.T, preferred_element_type=jnp.float32) + jnp.dot(value_grad, value_matrix.T, preferred_element_type=jnp.float32)).astype(jnp.bfloat16)
        out_total = out_total.at[positions].add(expert_out.astype(jnp.float32) * in_use)
        grad_total = grad_total.at[positions].add(row_grad.astype(jnp.float32) * in_use)
        return (out_total, grad_total)
    empty = jnp.zeros((TOKENS * TOP, L), jnp.float32)
    out_total, grad_total = lax.fori_loop(0, EXPERTS, per_expert, (empty, empty))
    combined = lax.optimization_barrier(jnp.sum(gate_values[:, :, None] * out_total.reshape(TOKENS, TOP, L), axis=1)).astype(jnp.bfloat16)
    latent_grad = lax.optimization_barrier(jnp.sum(grad_total.reshape(TOKENS, TOP, L), axis=1)).astype(jnp.bfloat16)
    grad_x = jnp.dot(down_proj, latent_grad.T, preferred_element_type=jnp.float32).astype(jnp.bfloat16)
    grad_down = jnp.dot(x_t, latent_grad, preferred_element_type=jnp.float32) * (1.0 / math.sqrt(TOKENS))
    return (combined, grad_x, grad_down)
```

```python
import math

import jax
import jax.numpy as jnp
from jax import lax
from jax.sharding import Mesh
from jax.sharding import PartitionSpec as P

f32 = jnp.float32
bf16 = jnp.bfloat16


def swap(blocks, axes):
    return lax.all_to_all(blocks, axes, split_axis=0, concat_axis=0, tiled=True)


def on_device(x_t, down_proj, w_gate, w_value, w_out, routes, gate_fix, cotangent):
    nx, ny, nc = lax.axis_size("x"), lax.axis_size("y"), lax.axis_size("c")
    nz = lax.axis_size("dp")
    groups = nx * ny * nc
    feats, width = down_proj.shape
    tokens = x_t.shape[1]
    tok_dev = tokens // groups
    block = tokens // nx
    top = routes.shape[1]
    capacity = max(2, 8 * tok_dev // groups)
    core = lax.axis_index("c")

    flat_routes = routes.reshape(-1)
    chosen = (flat_routes[:, None] == jnp.arange(groups, dtype=jnp.int32)[None, :]).astype(bf16)
    pairs = tok_dev * top
    earlier = (jnp.arange(pairs)[:, None] > jnp.arange(pairs)[None, :]).astype(bf16)
    before = jnp.dot(earlier, chosen, preferred_element_type=f32)
    slot_index = jnp.sum(before * chosen.astype(f32), axis=1).astype(jnp.int32)
    target = flat_routes * capacity + slot_index

    pieces = jnp.transpose(x_t.reshape(feats, nx, block), (1, 0, 2))
    packed = jnp.concatenate(
        [pieces, jnp.broadcast_to(down_proj[None], (nx, feats, width))], axis=2
    )
    packed = swap(packed, "x").reshape(nx * feats, block + width)
    both = lax.all_gather(packed, "c", axis=0, tiled=True)
    partial = lax.dot_general(
        both[:, :block], both[:, block:], (((0,), (0,)), ((), ())), preferred_element_type=f32
    ).astype(bf16)
    partial = partial.reshape(ny, nc, tok_dev, width)
    partial = lax.dynamic_index_in_dim(partial, core, axis=1, keepdims=False)
    latent = jnp.sum(swap(partial, "y").astype(f32), axis=0).astype(bf16)

    slots = groups * capacity
    hit = jnp.arange(slots, dtype=jnp.int32)[:, None] == target[None, :]
    gate_values = gate_fix.astype(f32) / 65536.0
    slot_gate = jnp.sum(jnp.where(hit, gate_values.reshape(1, -1), 0.0), axis=1)
    placing = jnp.sum(hit.reshape(slots, tok_dev, top).astype(f32), axis=2).astype(bf16)
    send_rows = jnp.dot(placing, latent, preferred_element_type=f32).astype(bf16)
    send_grads = slot_gate[:, None] * jnp.dot(placing, cotangent, preferred_element_type=f32)
    send = jnp.concatenate(
        [
            send_rows.reshape(groups, capacity, width),
            send_grads.astype(bf16).reshape(groups, capacity, width),
        ],
        axis=1,
    )
    got = swap(send, ("x", "y", "c"))
    rows = got[:, :capacity].reshape(slots, width)
    grads = got[:, capacity:].reshape(slots, width)

    gate_matrix, value_matrix, out_matrix = w_gate[0], w_value[0], w_out[0]
    last = (((1,), (1,)), ((), ()))
    pre_gate = jnp.dot(rows, gate_matrix, preferred_element_type=f32)
    pre_value = jnp.dot(rows, value_matrix, preferred_element_type=f32)
    sigmoid_gate = jax.nn.sigmoid(pre_gate)
    activated = pre_gate * sigmoid_gate
    hidden = (activated * pre_value).astype(bf16)
    expert_out = jnp.dot(hidden, out_matrix, preferred_element_type=f32).astype(bf16)
    hidden_grad = lax.dot_general(grads, out_matrix, last, preferred_element_type=f32)
    gate_grad = (
        hidden_grad * pre_value * sigmoid_gate * (1.0 + pre_gate * (1.0 - sigmoid_gate))
    ).astype(bf16)
    value_grad = (hidden_grad * activated).astype(bf16)
    row_grad = lax.dot_general(gate_grad, gate_matrix, last, preferred_element_type=f32)
    row_grad += lax.dot_general(value_grad, value_matrix, last, preferred_element_type=f32)
    reply = jnp.concatenate(
        [
            expert_out.reshape(groups, capacity, width),
            row_grad.astype(bf16).reshape(groups, capacity, width),
        ],
        axis=1,
    )
    back = swap(reply, ("x", "y", "c")).reshape(groups * 2 * capacity, width)

    place = jnp.arange(2 * slots, dtype=jnp.int32)
    low_slot = (place // (2 * capacity)) * capacity + place % capacity
    is_grad = (place // capacity) % 2 == 1
    spread = (low_slot[None, None, :] == target.reshape(tok_dev, top)[:, :, None]).astype(f32)
    high = jnp.sum(spread * (gate_fix // 256).astype(f32)[:, :, None], axis=1)
    low = jnp.sum(spread * (gate_fix % 256).astype(f32)[:, :, None], axis=1)
    one = jnp.sum(spread, axis=1)
    chooser = jnp.concatenate(
        [
            jnp.where(is_grad, 0.0, high * (1.0 / 256.0)),
            jnp.where(is_grad, 0.0, low * (1.0 / 65536.0)),
            jnp.where(is_grad, one, 0.0),
        ],
        axis=0,
    ).astype(bf16)
    summed = jnp.dot(chooser, back, preferred_element_type=f32)
    combined = (summed[:tok_dev] + summed[tok_dev : 2 * tok_dev]).astype(bf16)
    latent_grad = summed[2 * tok_dev :].astype(bf16)

    by_y = swap(jnp.broadcast_to(latent_grad[None], (ny, tok_dev, width)), "y")
    by_core = lax.all_gather(by_y, "c", axis=0, tiled=False)
    block_grad = jnp.transpose(by_core, (1, 0, 2, 3)).reshape(block, width)

    own_x, own_proj = packed[:, :block], packed[:, block:]
    scale = 1.0 / math.sqrt(tokens * nz)
    weight_part = jnp.dot(own_x, block_grad, preferred_element_type=f32) * scale
    input_part = lax.dot_general(own_proj, block_grad, last, preferred_element_type=f32)
    packed_back = jnp.concatenate([input_part.astype(bf16), weight_part.astype(bf16)], axis=1)
    packed_back = swap(packed_back.reshape(nx, feats, block + width), "x")
    grad_x = jnp.transpose(packed_back[:, :, :block], (1, 0, 2)).reshape(feats, tokens)
    weight_sum = jnp.sum(packed_back[:, :, block:].astype(f32), axis=0).astype(bf16)

    own_rows = swap(weight_sum.reshape(nz, feats // nz, width), "dp")
    own_rows = jnp.sum(own_rows.astype(f32), axis=0).astype(bf16)
    grad_down = swap(jnp.broadcast_to(own_rows[None], (nz, feats // nz, width)), "dp")
    grad_down = grad_down.reshape(feats, width).astype(f32)
    return (combined, grad_x, grad_down)


def solution(mesh):
    dp = mesh.shape["dp"]
    core = 2
    ny = 8
    nx = mesh.shape["expert"] // (ny * core)
    fine = Mesh(mesh.devices.reshape(nx, ny, core, dp), ("x", "y", "c", "dp"))
    expert = ("x", "y", "c")
    tokens = ("dp", "x", "y", "c")
    placed = (
        P(expert, "dp"),
        P(expert, None),
        P(expert, None, None),
        P(expert, None, None),
        P(expert, None, None),
        P(tokens, None),
        P(tokens, None),
        P(tokens, None),
    )
    return jax.shard_map(
        on_device,
        mesh=fine,
        in_specs=placed,
        out_specs=(P(tokens, None), P(expert, "dp"), P(expert, None)),
        check_vma=False,
    )
```

```python
import functools
import math

import jax
import jax.numpy as jnp
from jax import lax
from jax.experimental import pallas as pl
from jax.experimental.pallas import tpu as pltpu
from jax.sharding import Mesh
from jax.sharding import PartitionSpec as P

f32 = jnp.float32
bf16 = jnp.bfloat16
MiB = 1 << 20
last = (((1,), (1,)), ((), ()))
first = (((0,), (0,)), ((), ()))


def swap(blocks, axes):
    return lax.all_to_all(blocks, axes, split_axis=0, concat_axis=0, tiled=True)


def local(body, outs, *args, specs=None, limit=8, **static):
    vmem = pl.BlockSpec(memory_space=pltpu.VMEM)
    return pl.pallas_call(
        functools.partial(body, **static) if static else body,
        out_shape=outs,
        in_specs=[vmem] * len(args) if specs is None else specs,
        out_specs=jax.tree.map(lambda _: vmem, outs),
        compiler_params=pltpu.CompilerParams(vmem_limit_bytes=limit * MiB),
    )(*args)


def shape(*dims, dtype=bf16):
    return jax.ShapeDtypeStruct(dims, dtype)


def pack_body(x_ref, proj_ref, out_ref):
    pieces, _, wide = out_ref.shape
    block = wide - proj_ref.shape[1]
    for j in range(pieces):
        out_ref[j, :, :block] = x_ref[:, j * block : (j + 1) * block]
        out_ref[j, :, block:] = proj_ref[...]


def project_body(core_ref, own_ref, other_ref, out_ref):
    ny, rows, width = out_ref.shape
    block = own_ref.shape[1] - width
    part = lax.dot_general(
        own_ref[:, :block], own_ref[:, block:], first, preferred_element_type=f32
    )
    part += lax.dot_general(
        other_ref[:, :block], other_ref[:, block:], first, preferred_element_type=f32
    )
    part = part.reshape(ny, 2, rows, width)
    mine = jnp.where(core_ref[0] == 0, part[:, 0], part[:, 1])
    out_ref[...] = mine.astype(bf16)


def dispatch_body(parts_ref, cot_ref, place_ref, out_ref):
    half = out_ref.shape[1]
    latent = jnp.sum(parts_ref[...].astype(f32), axis=0).astype(bf16)
    cot = cot_ref[...]
    table = jnp.concatenate([latent[:, :half], latent[:, half:], cot[:, :half], cot[:, half:]], 0)
    place = place_ref[...]
    chosen = jnp.where(place != 0.0, 1.0, 0.0).astype(bf16)
    scale = jnp.sum(place, axis=1, keepdims=True)
    rows = jnp.dot(chosen, table, preferred_element_type=f32)
    out_ref[...] = (rows * scale).astype(bf16)


def expert_body(got_ref, gate_ref, value_ref, outw_ref, reply_ref):
    total, half = got_ref.shape
    chunk = 256
    devices = chunk // 8
    to = lax.broadcasted_iota(jnp.int32, (chunk, chunk), 0)
    source = lax.broadcasted_iota(jnp.int32, (chunk, chunk), 1)
    order = jnp.where((to % devices) * 8 + to // devices == source, 1.0, 0.0).astype(bf16)
    sorted_rows = [
        jnp.dot(order, got_ref[c * chunk : (c + 1) * chunk, :], preferred_element_type=f32).astype(
            bf16
        )
        for c in range(total // chunk)
    ]

    def matrix(kind):
        halves = []
        for h in range(2):
            pieces = []
            for piece in sorted_rows:
                for s in range(2):
                    r = (kind * 2 + s) * 2 + h
                    pieces.append(piece[r * devices : (r + 1) * devices])
            halves.append(jnp.concatenate(pieces, axis=0))
        return jnp.concatenate(halves, axis=1)

    rows, grads = matrix(0), matrix(1)
    pre_gate = jnp.dot(rows, gate_ref[0], preferred_element_type=f32)
    pre_value = jnp.dot(rows, value_ref[0], preferred_element_type=f32)
    hidden_grad = lax.dot_general(grads, outw_ref[0], last, preferred_element_type=f32)
    sigmoid_gate = jax.nn.sigmoid(pre_gate)
    activated = pre_gate * sigmoid_gate
    hidden = (activated * pre_value).astype(bf16)
    gate_grad = (
        hidden_grad * pre_value * sigmoid_gate * (1.0 + pre_gate * (1.0 - sigmoid_gate))
    ).astype(bf16)
    value_grad = (hidden_grad * activated).astype(bf16)
    expert_out = jnp.dot(hidden, outw_ref[0], preferred_element_type=f32).astype(bf16)
    row_grad = lax.dot_general(gate_grad, gate_ref[0], last, preferred_element_type=f32)
    row_grad += lax.dot_general(value_grad, value_ref[0], last, preferred_element_type=f32)
    row_grad = row_grad.astype(bf16)
    for c in range(total // chunk):
        pieces = []
        for kind in (expert_out, row_grad):
            for s in range(2):
                at = (c * 2 + s) * devices
                for h in range(2):
                    pieces.append(kind[at : at + devices, h * half : (h + 1) * half])
        stacked = jnp.concatenate(pieces, axis=0)
        reply_ref[c * chunk : (c + 1) * chunk, :] = lax.dot_general(
            order, stacked, first, preferred_element_type=f32
        ).astype(bf16)


def combine_body(back_ref, chooser_ref, combined_ref, spread_ref):
    copies, rows, width = spread_ref.shape
    half = width // 2
    summed = jnp.dot(chooser_ref[...], back_ref[...], preferred_element_type=f32)
    for h in range(2):
        lanes = slice(h * half, (h + 1) * half)
        at = 3 * rows * h
        high, low = summed[at : at + rows], summed[at + rows : at + 2 * rows]
        combined_ref[:, lanes] = (high + low).astype(bf16)
        grad = summed[at + 2 * rows : at + 3 * rows].astype(bf16)
        for j in range(copies):
            spread_ref[j, :, lanes] = grad


def backward_body(grad_ref, packed_ref, out_ref, *, scale):
    cores, ny, rows, width = grad_ref.shape
    block = cores * ny * rows
    grads = jnp.concatenate([grad_ref[c, y] for y in range(ny) for c in range(cores)], axis=0)
    out_ref[:, :block] = lax.dot_general(
        packed_ref[:, block:], grads, last, preferred_element_type=f32
    ).astype(bf16)
    weight = jnp.dot(packed_ref[:, :block], grads, preferred_element_type=f32)
    out_ref[:, block:] = (weight * scale).astype(bf16)


def gather_body(parts_ref, grad_x_ref, weight_ref):
    nx, feats, wide = parts_ref.shape
    block = grad_x_ref.shape[1] // nx
    tiles, tall, half = weight_ref.shape
    for j in range(nx):
        grad_x_ref[:, j * block : (j + 1) * block] = parts_ref[j, :, :block]
    total = jnp.sum(parts_ref[:, :, block:].astype(f32), axis=0).astype(bf16)
    for i in range(tiles):
        a, b = i // 2, i % 2
        weight_ref[i] = total[a * tall : (a + 1) * tall, b * half : (b + 1) * half]


def sum_body(parts_ref, out_ref):
    total = jnp.sum(parts_ref[...].astype(f32), axis=0).astype(bf16)
    out_ref[...] = jnp.broadcast_to(total[None], out_ref.shape)


def finish_body(tiles_ref, out_ref):
    tiles, tall, half = tiles_ref.shape
    for i in range(tiles):
        a, b = i // 2, i % 2
        out_ref[a * tall : (a + 1) * tall, b * half : (b + 1) * half] = tiles_ref[i].astype(f32)


def on_device(x_t, down_proj, w_gate, w_value, w_out, routes, gate_fix, cotangent):
    nx, ny, nc = lax.axis_size("x"), lax.axis_size("y"), lax.axis_size("c")
    nz = lax.axis_size("dp")
    groups = nx * ny * nc
    feats, width = down_proj.shape
    half = width // 2
    tokens = x_t.shape[1]
    tok_dev = tokens // groups
    block = tokens // nx
    top = routes.shape[1]
    pairs = tok_dev * top
    core = lax.axis_index("c").astype(jnp.int32).reshape(1)
    spec = pl.BlockSpec(memory_space=pltpu.VMEM)

    packed = local(pack_body, shape(nx, feats, block + width), x_t, down_proj)
    packed = swap(packed, "x").reshape(nx * feats, block + width)
    other = lax.ppermute(packed, "c", [(0, 1), (1, 0)])
    partial = local(
        project_body,
        shape(ny, tok_dev, width),
        core,
        packed,
        other,
        specs=[pl.BlockSpec(memory_space=pltpu.SMEM), spec, spec],
    )
    parts = swap(partial, "y")

    flat = routes.reshape(-1)
    chosen = (flat[:, None] == jnp.arange(groups, dtype=jnp.int32)[None, :]).astype(bf16)
    earlier = (jnp.arange(pairs)[:, None] > jnp.arange(pairs)[None, :]).astype(bf16)
    before = jnp.dot(earlier, chosen, preferred_element_type=f32)
    slot_index = jnp.sum(before * chosen.astype(f32), axis=1).astype(jnp.int32)
    target = (flat * 2 + slot_index).reshape(tok_dev, top)

    place = jnp.arange(groups * 8, dtype=jnp.int32)
    slot, kind, part = place // 8 * 2 + place % 4 // 2, place % 8 // 4, place % 2
    hit = slot[:, None, None] == target[None]
    gate_values = gate_fix.astype(f32) / 65536.0
    held = jnp.sum(jnp.where(hit, 1.0, 0.0), axis=2)
    gated = jnp.sum(jnp.where(hit, gate_values[None], 0.0), axis=2)
    where = jnp.concatenate(
        [
            jnp.where((kind == q // 2) & (part == q % 2), 1.0, 0.0)[:, None]
            * (held if q < 2 else gated)
            for q in range(4)
        ],
        axis=1,
    )
    spread = jnp.where(target[:, :, None] == slot[None, None, :], 1.0, 0.0)
    high = jnp.sum(spread * (gate_fix // 256).astype(f32)[:, :, None], axis=1) * (1.0 / 256.0)
    low = jnp.sum(spread * (gate_fix % 256).astype(f32)[:, :, None], axis=1) * (1.0 / 65536.0)
    one = jnp.sum(spread, axis=1)
    chooser = jnp.concatenate(
        [
            jnp.where(((kind == k) & (part == h))[None, :], value, 0.0)
            for h in range(2)
            for k, value in ((0, high), (0, low), (1, one))
        ],
        axis=0,
    ).astype(bf16)

    send = local(dispatch_body, shape(groups * 8, half), parts, cotangent, where)
    got = swap(send.reshape(groups, 8, half), ("x", "y", "c")).reshape(groups * 8, half)
    reply = local(
        expert_body, shape(groups * 8, half), got, w_gate, w_value, w_out, limit=32
    )
    back = swap(reply.reshape(groups, 8, half), ("x", "y", "c")).reshape(groups * 8, half)
    combined, by_owner = local(
        combine_body, (shape(tok_dev, width), shape(ny, tok_dev, width)), back, chooser
    )

    by_y = swap(by_owner, "y")
    by_core = lax.all_gather(by_y, "c", axis=0, tiled=False)
    packed_back = local(
        backward_body,
        shape(nx * feats, block + width),
        by_core,
        packed,
        scale=1.0 / math.sqrt(tokens * nz),
    )
    packed_back = swap(packed_back.reshape(nx, feats, block + width), "x")
    grad_x, weight_tiles = local(
        gather_body, (shape(feats, tokens), shape(16, feats // 8, half)), packed_back
    )

    tall = 16 // nz * feats // 8
    own = swap(weight_tiles.reshape(nz, tall, half), "dp")
    own = local(sum_body, shape(nz, tall, half), own)
    tiles = swap(own, "dp").reshape(16, feats // 8, half)
    grad_down = local(finish_body, shape(feats, width, dtype=f32), tiles)
    return (combined, grad_x, grad_down)


def solution(mesh):
    dp = mesh.shape["dp"]
    core = 2
    ny = 8
    nx = mesh.shape["expert"] // (ny * core)
    fine = Mesh(mesh.devices.reshape(nx, ny, core, dp), ("x", "y", "c", "dp"))
    expert = ("x", "y", "c")
    tokens = ("dp", "x", "y", "c")
    placed = (
        P(expert, "dp"),
        P(expert, None),
        P(expert, None, None),
        P(expert, None, None),
        P(expert, None, None),
        P(tokens, None),
        P(tokens, None),
        P(tokens, None),
    )
    return jax.shard_map(
        on_device,
        mesh=fine,
        in_specs=placed,
        out_specs=(P(tokens, None), P(expert, "dp"), P(expert, None)),
        check_vma=False,
    )
```

```python
import functools
import math

import jax
import jax.numpy as jnp
from jax import lax
from jax.experimental import pallas as pl
from jax.experimental.pallas import tpu as pltpu
from jax.sharding import Mesh
from jax.sharding import PartitionSpec as P

f32 = jnp.float32
bf16 = jnp.bfloat16
MiB = 1 << 20
last = (((1,), (1,)), ((), ()))
first = (((0,), (0,)), ((), ()))


def swap(blocks, axes):
    return lax.all_to_all(blocks, axes, split_axis=0, concat_axis=0, tiled=True)


vmem = pl.BlockSpec(memory_space=pltpu.VMEM)
smem = pl.BlockSpec(memory_space=pltpu.SMEM)
anywhere = pl.BlockSpec(memory_space=pl.ANY)
hbm = pl.BlockSpec(memory_space=pltpu.HBM)


def local(body, outs, *args, specs=None, out_spec=vmem, scratch=(), limit=8, **static):
    return pl.pallas_call(
        functools.partial(body, **static) if static else body,
        out_shape=outs,
        in_specs=[vmem] * len(args) if specs is None else specs,
        out_specs=jax.tree.map(lambda _: out_spec, outs),
        scratch_shapes=list(scratch),
        compiler_params=pltpu.CompilerParams(vmem_limit_bytes=limit * MiB),
    )(*args)


def shape(*dims, dtype=bf16):
    return jax.ShapeDtypeStruct(dims, dtype)


def pack_body(x_ref, proj_ref, out_ref, sems):
    pieces, _, wide = out_ref.shape
    block = wide - proj_ref.shape[1]
    copies = []
    for j in range(pieces):
        copies.append(
            pltpu.make_async_copy(
                x_ref.at[:, pl.ds(j * block, block)],
                out_ref.at[j, :, pl.ds(0, block)],
                sems.at[2 * j],
            )
        )
        copies.append(
            pltpu.make_async_copy(
                proj_ref, out_ref.at[j, :, pl.ds(block, wide - block)], sems.at[2 * j + 1]
            )
        )
    for copy in copies:
        copy.start()
    for copy in copies:
        copy.wait()


def project_body(core_ref, packed_ref, mine_ref, theirs_ref):
    ny, rows, width = mine_ref.shape
    block = packed_ref.shape[1] - width
    part = lax.dot_general(
        packed_ref[:, :block], packed_ref[:, block:], first, preferred_element_type=f32
    )
    part = part.astype(bf16).reshape(ny, 2, rows, width)
    even = core_ref[0] == 0
    mine_ref[...] = jnp.where(even, part[:, 0], part[:, 1])
    theirs_ref[...] = jnp.where(even, part[:, 1], part[:, 0])


def add_body(core_ref, mine_ref, sent_ref, out_ref):
    other = jnp.where(core_ref[0] == 0, sent_ref[1], sent_ref[0])
    out_ref[...] = (mine_ref[...].astype(f32) + other.astype(f32)).astype(bf16)


def dispatch_body(parts_ref, cot_ref, place_ref, _chooser, out_ref):
    half = out_ref.shape[1]
    latent = jnp.sum(parts_ref[...].astype(f32), axis=0).astype(bf16)
    cot = cot_ref[...]
    table = jnp.concatenate([latent[:, :half], latent[:, half:], cot[:, :half], cot[:, half:]], 0)
    place = place_ref[...]
    chosen = jnp.where(place != 0.0, 1.0, 0.0).astype(bf16)
    scale = jnp.sum(place, axis=1, keepdims=True)
    rows = jnp.dot(chosen, table, preferred_element_type=f32)
    out_ref[...] = (rows * scale).astype(bf16)


def expert_body(got_ref, gate_ref, value_ref, outw_ref, reply_ref):
    total, half = got_ref.shape
    chunk = 256
    devices = chunk // 8
    to = lax.broadcasted_iota(jnp.int32, (chunk, chunk), 0)
    source = lax.broadcasted_iota(jnp.int32, (chunk, chunk), 1)
    order = jnp.where((to % devices) * 8 + to // devices == source, 1.0, 0.0).astype(bf16)
    sorted_rows = [
        jnp.dot(order, got_ref[c * chunk : (c + 1) * chunk, :], preferred_element_type=f32).astype(
            bf16
        )
        for c in range(total // chunk)
    ]

    def matrix(kind):
        halves = []
        for h in range(2):
            pieces = []
            for piece in sorted_rows:
                for s in range(2):
                    r = (kind * 2 + s) * 2 + h
                    pieces.append(piece[r * devices : (r + 1) * devices])
            halves.append(jnp.concatenate(pieces, axis=0))
        return jnp.concatenate(halves, axis=1)

    rows, grads = matrix(0), matrix(1)
    pre_gate = jnp.dot(rows, gate_ref[0], preferred_element_type=f32)
    pre_value = jnp.dot(rows, value_ref[0], preferred_element_type=f32)
    hidden_grad = lax.dot_general(grads, outw_ref[0], last, preferred_element_type=f32)
    sigmoid_gate = jax.nn.sigmoid(pre_gate)
    activated = pre_gate * sigmoid_gate
    hidden = (activated * pre_value).astype(bf16)
    gate_grad = (
        hidden_grad * pre_value * sigmoid_gate * (1.0 + pre_gate * (1.0 - sigmoid_gate))
    ).astype(bf16)
    value_grad = (hidden_grad * activated).astype(bf16)
    expert_out = jnp.dot(hidden, outw_ref[0], preferred_element_type=f32).astype(bf16)
    row_grad = lax.dot_general(gate_grad, gate_ref[0], last, preferred_element_type=f32)
    row_grad += lax.dot_general(value_grad, value_ref[0], last, preferred_element_type=f32)
    row_grad = row_grad.astype(bf16)
    for c in range(total // chunk):
        pieces = []
        for kind in (expert_out, row_grad):
            for s in range(2):
                at = (c * 2 + s) * devices
                for h in range(2):
                    pieces.append(kind[at : at + devices, h * half : (h + 1) * half])
        stacked = jnp.concatenate(pieces, axis=0)
        reply_ref[c * chunk : (c + 1) * chunk, :] = lax.dot_general(
            order, stacked, first, preferred_element_type=f32
        ).astype(bf16)


def combine_body(back_ref, chooser_ref, combined_ref, spread_ref):
    copies, rows, width = spread_ref.shape
    half = width // 2
    summed = jnp.dot(chooser_ref[...], back_ref[...], preferred_element_type=f32)
    for h in range(2):
        lanes = slice(h * half, (h + 1) * half)
        at = 3 * rows * h
        high, low = summed[at : at + rows], summed[at + rows : at + 2 * rows]
        combined_ref[:, lanes] = (high + low).astype(bf16)
        grad = summed[at + 2 * rows : at + 3 * rows].astype(bf16)
        for j in range(copies):
            spread_ref[j, :, lanes] = grad


def backward_body(grad_ref, packed_ref, out_ref, *, scale):
    cores, ny, rows, width = grad_ref.shape
    block = cores * ny * rows
    grads = jnp.concatenate([grad_ref[c, y] for y in range(ny) for c in range(cores)], axis=0)
    out_ref[:, :block] = lax.dot_general(
        packed_ref[:, block:], grads, last, preferred_element_type=f32
    ).astype(bf16)
    weight = jnp.dot(packed_ref[:, :block], grads, preferred_element_type=f32)
    out_ref[:, block:] = (weight * scale).astype(bf16)


def gather_body(parts_ref, grad_x_ref, weight_ref):
    nx, feats, wide = parts_ref.shape
    block = grad_x_ref.shape[1] // nx
    tiles, tall, half = weight_ref.shape
    for j in range(nx):
        grad_x_ref[:, j * block : (j + 1) * block] = parts_ref[j, :, :block]
    total = jnp.sum(parts_ref[:, :, block:].astype(f32), axis=0).astype(bf16)
    for i in range(tiles):
        a, b = i // 2, i % 2
        weight_ref[i] = total[a * tall : (a + 1) * tall, b * half : (b + 1) * half]


def sum_body(parts_ref, out_ref):
    total = jnp.sum(parts_ref[...].astype(f32), axis=0).astype(bf16)
    out_ref[...] = jnp.broadcast_to(total[None], out_ref.shape)


def finish_body(tiles_ref, out_ref):
    tiles, tall, half = tiles_ref.shape
    for i in range(tiles):
        a, b = i // 2, i % 2
        out_ref[a * tall : (a + 1) * tall, b * half : (b + 1) * half] = tiles_ref[i].astype(f32)


def on_device(x_t, down_proj, w_gate, w_value, w_out, routes, gate_fix, cotangent):
    nx, ny, nc = lax.axis_size("x"), lax.axis_size("y"), lax.axis_size("c")
    nz = lax.axis_size("dp")
    groups = nx * ny * nc
    feats, width = down_proj.shape
    half = width // 2
    tokens = x_t.shape[1]
    tok_dev = tokens // groups
    block = tokens // nx
    top = routes.shape[1]
    pairs = tok_dev * top
    core = lax.axis_index("c").astype(jnp.int32).reshape(1)

    packed = local(
        pack_body,
        shape(nx, feats, block + width),
        x_t,
        down_proj,
        specs=[hbm, hbm],
        scratch=[pltpu.SemaphoreType.DMA((2 * nx,))],
        limit=60,
    )
    packed = swap(packed, "x").reshape(nx * feats, block + width)
    mine, theirs = local(
        project_body,
        (shape(ny, tok_dev, width), shape(ny, tok_dev, width)),
        core,
        packed,
        specs=[smem, vmem],
    )
    sent = lax.all_gather(theirs, "c", axis=0, tiled=False)
    partial = local(
        add_body, shape(ny, tok_dev, width), core, mine, sent, specs=[smem, vmem, vmem]
    )
    parts = swap(partial, "y")

    flat = routes.reshape(-1)
    chosen = (flat[:, None] == jnp.arange(groups, dtype=jnp.int32)[None, :]).astype(bf16)
    earlier = (jnp.arange(pairs)[:, None] > jnp.arange(pairs)[None, :]).astype(bf16)
    before = jnp.dot(earlier, chosen, preferred_element_type=f32)
    slot_index = jnp.sum(before * chosen.astype(f32), axis=1).astype(jnp.int32)
    target = (flat * 2 + slot_index).reshape(tok_dev, top)

    place = jnp.arange(groups * 8, dtype=jnp.int32)
    slot, kind, part = place // 8 * 2 + place % 4 // 2, place % 8 // 4, place % 2
    hit = slot[:, None, None] == target[None]
    gate_values = gate_fix.astype(f32) / 65536.0
    held = jnp.sum(jnp.where(hit, 1.0, 0.0), axis=2)
    gated = jnp.sum(jnp.where(hit, gate_values[None], 0.0), axis=2)
    where = jnp.concatenate(
        [
            jnp.where((kind == q // 2) & (part == q % 2), 1.0, 0.0)[:, None]
            * (held if q < 2 else gated)
            for q in range(4)
        ],
        axis=1,
    )
    spread = jnp.where(target[:, :, None] == slot[None, None, :], 1.0, 0.0)
    high = jnp.sum(spread * (gate_fix // 256).astype(f32)[:, :, None], axis=1) * (1.0 / 256.0)
    low = jnp.sum(spread * (gate_fix % 256).astype(f32)[:, :, None], axis=1) * (1.0 / 65536.0)
    one = jnp.sum(spread, axis=1)
    chooser = jnp.concatenate(
        [
            jnp.where(((kind == k) & (part == h))[None, :], value, 0.0)
            for h in range(2)
            for k, value in ((0, high), (0, low), (1, one))
        ],
        axis=0,
    ).astype(bf16)

    send = local(
        dispatch_body,
        shape(groups * 8, half),
        parts,
        cotangent,
        where,
        chooser,
        specs=[vmem, vmem, vmem, anywhere],
    )
    got = swap(send.reshape(groups, 8, half), ("x", "y", "c")).reshape(groups * 8, half)
    reply = local(
        expert_body,
        shape(groups * 8, half),
        got,
        w_gate,
        w_value,
        w_out,
        limit=24,
    )
    back = swap(reply.reshape(groups, 8, half), ("x", "y", "c")).reshape(groups * 8, half)
    combined, by_owner = local(
        combine_body, (shape(tok_dev, width), shape(ny, tok_dev, width)), back, chooser
    )

    by_y = swap(by_owner, "y")
    by_core = lax.all_gather(by_y, "c", axis=0, tiled=False)
    packed_back = local(
        backward_body,
        shape(nx * feats, block + width),
        by_core,
        packed,
        scale=1.0 / math.sqrt(tokens * nz),
    )
    packed_back = swap(packed_back.reshape(nx, feats, block + width), "x")
    grad_x, weight_tiles = local(
        gather_body, (shape(feats, tokens), shape(16, feats // 8, half)), packed_back
    )

    tall = 16 // nz * feats // 8
    own = swap(weight_tiles.reshape(nz, tall, half), "dp")
    own = local(sum_body, shape(nz, tall, half), own)
    tiles = swap(own, "dp").reshape(16, feats // 8, half)
    grad_down = local(finish_body, shape(feats, width, dtype=f32), tiles)
    return (combined, grad_x, grad_down)


def solution(mesh):
    dp = mesh.shape["dp"]
    core = 2
    ny = 8
    nx = mesh.shape["expert"] // (ny * core)
    fine = Mesh(mesh.devices.reshape(nx, ny, core, dp), ("x", "y", "c", "dp"))
    expert = ("x", "y", "c")
    tokens = ("dp", "x", "y", "c")
    placed = (
        P(expert, "dp"),
        P(expert, None),
        P(expert, None, None),
        P(expert, None, None),
        P(expert, None, None),
        P(tokens, None),
        P(tokens, None),
        P(tokens, None),
    )
    return jax.shard_map(
        on_device,
        mesh=fine,
        in_specs=placed,
        out_specs=(P(tokens, None), P(expert, "dp"), P(expert, None)),
        check_vma=False,
    )
```

```python
import functools
import math

import jax
import jax.numpy as jnp
from jax import lax
from jax.experimental import pallas as pl
from jax.experimental.pallas import tpu as pltpu
from jax.sharding import Mesh
from jax.sharding import PartitionSpec as P

f32 = jnp.float32
bf16 = jnp.bfloat16
MiB = 1 << 20
last = (((1,), (1,)), ((), ()))
first = (((0,), (0,)), ((), ()))


def swap(blocks, axes):
    return lax.all_to_all(blocks, axes, split_axis=0, concat_axis=0, tiled=True)


vmem = pl.BlockSpec(memory_space=pltpu.VMEM)
smem = pl.BlockSpec(memory_space=pltpu.SMEM)
anywhere = pl.BlockSpec(memory_space=pl.ANY)
hbm = pl.BlockSpec(memory_space=pltpu.HBM)


def local(body, outs, *args, specs=None, out_spec=vmem, scratch=(), limit=8, **static):
    return pl.pallas_call(
        functools.partial(body, **static) if static else body,
        out_shape=outs,
        in_specs=[vmem] * len(args) if specs is None else specs,
        out_specs=jax.tree.map(lambda _: out_spec, outs),
        scratch_shapes=list(scratch),
        compiler_params=pltpu.CompilerParams(vmem_limit_bytes=limit * MiB),
    )(*args)


def shape(*dims, dtype=bf16):
    return jax.ShapeDtypeStruct(dims, dtype)


def pack_body(x_hbm, proj_hbm, out_ref, x_ref, proj_ref, sems):
    pieces, _, wide = out_ref.shape
    block = wide - proj_ref.shape[1]
    loads = [
        pltpu.make_async_copy(x_hbm, x_ref, sems.at[0]),
        pltpu.make_async_copy(proj_hbm, proj_ref, sems.at[1]),
    ]
    for load in loads:
        load.start()
    loads[0].wait()
    for j in range(pieces):
        out_ref[j, :, :block] = x_ref[:, j * block : (j + 1) * block]
    loads[1].wait()
    for j in range(pieces):
        out_ref[j, :, block:] = proj_ref[...]


def project_body(core_ref, packed_ref, mine_ref, theirs_ref):
    ny, rows, width = mine_ref.shape
    block = packed_ref.shape[1] - width
    part = lax.dot_general(
        packed_ref[:, :block], packed_ref[:, block:], first, preferred_element_type=f32
    )
    part = part.astype(bf16).reshape(ny, 2, rows, width)
    even = core_ref[0] == 0
    mine_ref[...] = jnp.where(even, part[:, 0], part[:, 1])
    theirs_ref[...] = jnp.where(even, part[:, 1], part[:, 0])


def add_body(core_ref, mine_ref, sent_ref, out_ref):
    other = jnp.where(core_ref[0] == 0, sent_ref[1], sent_ref[0])
    out_ref[...] = (mine_ref[...].astype(f32) + other.astype(f32)).astype(bf16)


def dispatch_body(parts_ref, cot_ref, place_ref, _chooser, out_ref):
    half = out_ref.shape[1]
    latent = jnp.sum(parts_ref[...].astype(f32), axis=0).astype(bf16)
    cot = cot_ref[...]
    table = jnp.concatenate([latent[:, :half], latent[:, half:], cot[:, :half], cot[:, half:]], 0)
    place = place_ref[...]
    chosen = jnp.where(place != 0.0, 1.0, 0.0).astype(bf16)
    scale = jnp.sum(place, axis=1, keepdims=True)
    rows = jnp.dot(chosen, table, preferred_element_type=f32)
    out_ref[...] = (rows * scale).astype(bf16)


def expert_body(
    got_ref, gate_ref, value_hbm, outw_hbm, reply_ref, value_ref, outw_ref, sems
):
    loads = []
    count = sems.shape[1]
    for i, (source, target) in enumerate(
        ((value_hbm, value_ref), (outw_hbm, outw_ref))
    ):
        tall = source.shape[1] // count
        loads.append(
            [
                pltpu.make_async_copy(
                    source.at[0, pl.ds(j * tall, tall)],
                    target.at[0, pl.ds(j * tall, tall)],
                    sems.at[i, j],
                )
                for j in range(count)
            ]
        )
    for group in loads:
        for load in group:
            load.start()

    def arrived(i):
        for load in loads[i]:
            load.wait()

    total, half = got_ref.shape
    chunk = 256
    devices = chunk // 8
    to = lax.broadcasted_iota(jnp.int32, (chunk, chunk), 0)
    source = lax.broadcasted_iota(jnp.int32, (chunk, chunk), 1)
    order = jnp.where((to % devices) * 8 + to // devices == source, 1.0, 0.0).astype(bf16)
    sorted_rows = [
        jnp.dot(order, got_ref[c * chunk : (c + 1) * chunk, :], preferred_element_type=f32).astype(
            bf16
        )
        for c in range(total // chunk)
    ]

    def matrix(kind):
        halves = []
        for h in range(2):
            pieces = []
            for piece in sorted_rows:
                for s in range(2):
                    r = (kind * 2 + s) * 2 + h
                    pieces.append(piece[r * devices : (r + 1) * devices])
            halves.append(jnp.concatenate(pieces, axis=0))
        return jnp.concatenate(halves, axis=1)

    rows, grads = matrix(0), matrix(1)
    pre_gate = jnp.dot(rows, gate_ref[0], preferred_element_type=f32)
    arrived(0)
    pre_value = jnp.dot(rows, value_ref[0], preferred_element_type=f32)
    arrived(1)
    hidden_grad = lax.dot_general(grads, outw_ref[0], last, preferred_element_type=f32)
    sigmoid_gate = jax.nn.sigmoid(pre_gate)
    activated = pre_gate * sigmoid_gate
    hidden = (activated * pre_value).astype(bf16)
    gate_grad = (
        hidden_grad * pre_value * sigmoid_gate * (1.0 + pre_gate * (1.0 - sigmoid_gate))
    ).astype(bf16)
    value_grad = (hidden_grad * activated).astype(bf16)
    expert_out = jnp.dot(hidden, outw_ref[0], preferred_element_type=f32).astype(bf16)
    row_grad = lax.dot_general(gate_grad, gate_ref[0], last, preferred_element_type=f32)
    row_grad += lax.dot_general(value_grad, value_ref[0], last, preferred_element_type=f32)
    row_grad = row_grad.astype(bf16)
    for c in range(total // chunk):
        pieces = []
        for kind in (expert_out, row_grad):
            for s in range(2):
                at = (c * 2 + s) * devices
                for h in range(2):
                    pieces.append(kind[at : at + devices, h * half : (h + 1) * half])
        stacked = jnp.concatenate(pieces, axis=0)
        reply_ref[c * chunk : (c + 1) * chunk, :] = lax.dot_general(
            order, stacked, first, preferred_element_type=f32
        ).astype(bf16)


def combine_body(back_ref, chooser_ref, combined_ref, spread_ref):
    copies, rows, width = spread_ref.shape
    half = width // 2
    summed = jnp.dot(chooser_ref[...], back_ref[...], preferred_element_type=f32)
    for h in range(2):
        lanes = slice(h * half, (h + 1) * half)
        at = 3 * rows * h
        high, low = summed[at : at + rows], summed[at + rows : at + 2 * rows]
        combined_ref[:, lanes] = (high + low).astype(bf16)
        grad = summed[at + 2 * rows : at + 3 * rows].astype(bf16)
        for j in range(copies):
            spread_ref[j, :, lanes] = grad


def backward_body(grad_ref, packed_ref, out_ref, *, scale):
    cores, ny, rows, width = grad_ref.shape
    block = cores * ny * rows
    grads = jnp.concatenate([grad_ref[c, y] for y in range(ny) for c in range(cores)], axis=0)
    out_ref[:, :block] = lax.dot_general(
        packed_ref[:, block:], grads, last, preferred_element_type=f32
    ).astype(bf16)
    weight = jnp.dot(packed_ref[:, :block], grads, preferred_element_type=f32)
    out_ref[:, block:] = (weight * scale).astype(bf16)


def gather_body(parts_ref, grad_x_ref, weight_ref):
    nx, feats, wide = parts_ref.shape
    block = grad_x_ref.shape[1] // nx
    tiles, tall, half = weight_ref.shape
    for j in range(nx):
        grad_x_ref[:, j * block : (j + 1) * block] = parts_ref[j, :, :block]
    total = jnp.sum(parts_ref[:, :, block:].astype(f32), axis=0).astype(bf16)
    for i in range(tiles):
        a, b = i // 2, i % 2
        weight_ref[i] = total[a * tall : (a + 1) * tall, b * half : (b + 1) * half]


def sum_body(parts_ref, out_ref):
    total = jnp.sum(parts_ref[...].astype(f32), axis=0).astype(bf16)
    out_ref[...] = jnp.broadcast_to(total[None], out_ref.shape)


def finish_body(tiles_ref, out_ref):
    tiles, tall, half = tiles_ref.shape
    for i in range(tiles):
        a, b = i // 2, i % 2
        out_ref[a * tall : (a + 1) * tall, b * half : (b + 1) * half] = tiles_ref[i].astype(f32)


def on_device(x_t, down_proj, w_gate, w_value, w_out, routes, gate_fix, cotangent):
    nx, ny, nc = lax.axis_size("x"), lax.axis_size("y"), lax.axis_size("c")
    nz = lax.axis_size("dp")
    groups = nx * ny * nc
    feats, width = down_proj.shape
    half = width // 2
    tokens = x_t.shape[1]
    tok_dev = tokens // groups
    block = tokens // nx
    top = routes.shape[1]
    pairs = tok_dev * top
    core = lax.axis_index("c").astype(jnp.int32).reshape(1)

    packed = local(
        pack_body,
        shape(nx, feats, block + width),
        x_t,
        down_proj,
        specs=[hbm, hbm],
        scratch=[
            pltpu.VMEM(x_t.shape, bf16),
            pltpu.VMEM(down_proj.shape, bf16),
            pltpu.SemaphoreType.DMA((2,)),
        ],
        limit=60,
    )
    packed = swap(packed, "x").reshape(nx * feats, block + width)
    mine, theirs = local(
        project_body,
        (shape(ny, tok_dev, width), shape(ny, tok_dev, width)),
        core,
        packed,
        specs=[smem, vmem],
    )
    sent = lax.all_gather(theirs, "c", axis=0, tiled=False)
    partial = local(
        add_body, shape(ny, tok_dev, width), core, mine, sent, specs=[smem, vmem, vmem]
    )
    parts = swap(partial, "y")

    flat = routes.reshape(-1)
    chosen = (flat[:, None] == jnp.arange(groups, dtype=jnp.int32)[None, :]).astype(bf16)
    earlier = (jnp.arange(pairs)[:, None] > jnp.arange(pairs)[None, :]).astype(bf16)
    before = jnp.dot(earlier, chosen, preferred_element_type=f32)
    slot_index = jnp.sum(before * chosen.astype(f32), axis=1).astype(jnp.int32)
    target = (flat * 2 + slot_index).reshape(tok_dev, top)

    place = jnp.arange(groups * 8, dtype=jnp.int32)
    slot, kind, part = place // 8 * 2 + place % 4 // 2, place % 8 // 4, place % 2
    hit = slot[:, None, None] == target[None]
    gate_values = gate_fix.astype(f32) / 65536.0
    held = jnp.sum(jnp.where(hit, 1.0, 0.0), axis=2)
    gated = jnp.sum(jnp.where(hit, gate_values[None], 0.0), axis=2)
    where = jnp.concatenate(
        [
            jnp.where((kind == q // 2) & (part == q % 2), 1.0, 0.0)[:, None]
            * (held if q < 2 else gated)
            for q in range(4)
        ],
        axis=1,
    )
    spread = jnp.where(target[:, :, None] == slot[None, None, :], 1.0, 0.0)
    high = jnp.sum(spread * (gate_fix // 256).astype(f32)[:, :, None], axis=1) * (1.0 / 256.0)
    low = jnp.sum(spread * (gate_fix % 256).astype(f32)[:, :, None], axis=1) * (1.0 / 65536.0)
    one = jnp.sum(spread, axis=1)
    chooser = jnp.concatenate(
        [
            jnp.where(((kind == k) & (part == h))[None, :], value, 0.0)
            for h in range(2)
            for k, value in ((0, high), (0, low), (1, one))
        ],
        axis=0,
    ).astype(bf16)

    send = local(
        dispatch_body,
        shape(groups * 8, half),
        parts,
        cotangent,
        where,
        chooser,
        specs=[vmem, vmem, vmem, anywhere],
    )
    got = swap(send.reshape(groups, 8, half), ("x", "y", "c")).reshape(groups * 8, half)
    reply = local(
        expert_body,
        shape(groups * 8, half),
        got,
        w_gate,
        w_value,
        w_out,
        specs=[vmem, vmem, hbm, hbm],
        scratch=[
            pltpu.VMEM(w_value.shape, bf16),
            pltpu.VMEM(w_out.shape, bf16),
            pltpu.SemaphoreType.DMA((2, 4)),
        ],
        limit=50,
    )
    back = swap(reply.reshape(groups, 8, half), ("x", "y", "c")).reshape(groups * 8, half)
    combined, by_owner = local(
        combine_body, (shape(tok_dev, width), shape(ny, tok_dev, width)), back, chooser
    )

    by_y = swap(by_owner, "y")
    by_core = lax.all_gather(by_y, "c", axis=0, tiled=False)
    packed_back = local(
        backward_body,
        shape(nx * feats, block + width),
        by_core,
        packed,
        scale=1.0 / math.sqrt(tokens * nz),
    )
    packed_back = swap(packed_back.reshape(nx, feats, block + width), "x")
    grad_x, weight_tiles = local(
        gather_body, (shape(feats, tokens), shape(16, feats // 8, half)), packed_back
    )

    tall = 16 // nz * feats // 8
    own = swap(weight_tiles.reshape(nz, tall, half), "dp")
    own = local(sum_body, shape(nz, tall, half), own)
    tiles = swap(own, "dp").reshape(16, feats // 8, half)
    grad_down = local(finish_body, shape(feats, width, dtype=f32), tiles)
    return (combined, grad_x, grad_down)


def solution(mesh):
    dp = mesh.shape["dp"]
    core = 2
    ny = 8
    nx = mesh.shape["expert"] // (ny * core)
    fine = Mesh(mesh.devices.reshape(nx, ny, core, dp), ("x", "y", "c", "dp"))
    expert = ("x", "y", "c")
    tokens = ("dp", "x", "y", "c")
    placed = (
        P(expert, "dp"),
        P(expert, None),
        P(expert, None, None),
        P(expert, None, None),
        P(expert, None, None),
        P(tokens, None),
        P(tokens, None),
        P(tokens, None),
    )
    return jax.shard_map(
        on_device,
        mesh=fine,
        in_specs=placed,
        out_specs=(P(tokens, None), P(expert, "dp"), P(expert, None)),
        check_vma=False,
    )
```

```python
import functools
import math

import jax
import jax.numpy as jnp
from jax import lax
from jax.experimental import pallas as pl
from jax.experimental.pallas import tpu as pltpu
from jax.sharding import Mesh
from jax.sharding import PartitionSpec as P

f32 = jnp.float32
bf16 = jnp.bfloat16
MiB = 1 << 20
last = (((1,), (1,)), ((), ()))
first = (((0,), (0,)), ((), ()))


def swap(blocks, axes):
    return lax.all_to_all(blocks, axes, split_axis=0, concat_axis=0, tiled=True)


vmem = pl.BlockSpec(memory_space=pltpu.VMEM)
smem = pl.BlockSpec(memory_space=pltpu.SMEM)
anywhere = pl.BlockSpec(memory_space=pl.ANY)
hbm = pl.BlockSpec(memory_space=pltpu.HBM)


def local(body, outs, *args, specs=None, out_spec=vmem, scratch=(), limit=8, **static):
    return pl.pallas_call(
        functools.partial(body, **static) if static else body,
        out_shape=outs,
        in_specs=[vmem] * len(args) if specs is None else specs,
        out_specs=jax.tree.map(lambda _: out_spec, outs),
        scratch_shapes=list(scratch),
        compiler_params=pltpu.CompilerParams(vmem_limit_bytes=limit * MiB),
    )(*args)


def shape(*dims, dtype=bf16):
    return jax.ShapeDtypeStruct(dims, dtype)


def pack_body(x_hbm, proj_hbm, out_ref, x_ref, proj_ref, sems):
    pieces, _, wide = out_ref.shape
    block = wide - proj_ref.shape[1]
    loads = [
        pltpu.make_async_copy(x_hbm, x_ref, sems.at[0]),
        pltpu.make_async_copy(proj_hbm, proj_ref, sems.at[1]),
    ]
    for load in loads:
        load.start()
    loads[0].wait()
    for j in range(pieces):
        out_ref[j, :, :block] = x_ref[:, j * block : (j + 1) * block]
    loads[1].wait()
    for j in range(pieces):
        out_ref[j, :, block:] = proj_ref[...]


def project_body(core_ref, packed_ref, mine_ref, theirs_ref):
    ny, rows, width = mine_ref.shape
    block = packed_ref.shape[1] - width
    part = lax.dot_general(
        packed_ref[:, :block], packed_ref[:, block:], first, preferred_element_type=f32
    )
    part = part.astype(bf16).reshape(ny, 2, rows, width)
    even = core_ref[0] == 0
    mine_ref[...] = jnp.where(even, part[:, 0], part[:, 1])
    theirs_ref[...] = jnp.where(even, part[:, 1], part[:, 0])


def add_body(core_ref, mine_ref, sent_ref, _place, _chooser, out_ref):
    other = jnp.where(core_ref[0] == 0, sent_ref[1], sent_ref[0])
    out_ref[...] = (mine_ref[...].astype(f32) + other.astype(f32)).astype(bf16)


def dispatch_body(parts_ref, cot_ref, place_ref, out_ref):
    half = out_ref.shape[1]
    latent = jnp.sum(parts_ref[...].astype(f32), axis=0).astype(bf16)
    cot = cot_ref[...]
    table = jnp.concatenate([latent[:, :half], latent[:, half:], cot[:, :half], cot[:, half:]], 0)
    place = place_ref[...]
    chosen = jnp.where(place != 0.0, 1.0, 0.0).astype(bf16)
    scale = jnp.sum(place, axis=1, keepdims=True)
    rows = jnp.dot(chosen, table, preferred_element_type=f32)
    out_ref[...] = (rows * scale).astype(bf16)


def expert_body(
    got_ref, gate_ref, value_hbm, outw_hbm, reply_ref, value_ref, outw_ref, sems
):
    loads = []
    count = sems.shape[1]
    for i, (source, target) in enumerate(
        ((value_hbm, value_ref), (outw_hbm, outw_ref))
    ):
        tall = source.shape[1] // count
        loads.append(
            [
                pltpu.make_async_copy(
                    source.at[0, pl.ds(j * tall, tall)],
                    target.at[0, pl.ds(j * tall, tall)],
                    sems.at[i, j],
                )
                for j in range(count)
            ]
        )
    for group in loads:
        for load in group:
            load.start()

    def arrived(i):
        for load in loads[i]:
            load.wait()

    total, half = got_ref.shape
    chunk = 256
    devices = chunk // 8
    to = lax.broadcasted_iota(jnp.int32, (chunk, chunk), 0)
    source = lax.broadcasted_iota(jnp.int32, (chunk, chunk), 1)
    order = jnp.where((to % devices) * 8 + to // devices == source, 1.0, 0.0).astype(bf16)
    sorted_rows = [
        jnp.dot(order, got_ref[c * chunk : (c + 1) * chunk, :], preferred_element_type=f32).astype(
            bf16
        )
        for c in range(total // chunk)
    ]

    def matrix(kind):
        halves = []
        for h in range(2):
            pieces = []
            for piece in sorted_rows:
                for s in range(2):
                    r = (kind * 2 + s) * 2 + h
                    pieces.append(piece[r * devices : (r + 1) * devices])
            halves.append(jnp.concatenate(pieces, axis=0))
        return jnp.concatenate(halves, axis=1)

    rows, grads = matrix(0), matrix(1)
    pre_gate = jnp.dot(rows, gate_ref[0], preferred_element_type=f32)
    arrived(0)
    pre_value = jnp.dot(rows, value_ref[0], preferred_element_type=f32)
    arrived(1)
    hidden_grad = lax.dot_general(grads, outw_ref[0], last, preferred_element_type=f32)
    sigmoid_gate = jax.nn.sigmoid(pre_gate)
    activated = pre_gate * sigmoid_gate
    hidden = (activated * pre_value).astype(bf16)
    gate_grad = (
        hidden_grad * pre_value * sigmoid_gate * (1.0 + pre_gate * (1.0 - sigmoid_gate))
    ).astype(bf16)
    value_grad = (hidden_grad * activated).astype(bf16)
    expert_out = jnp.dot(hidden, outw_ref[0], preferred_element_type=f32).astype(bf16)
    row_grad = lax.dot_general(gate_grad, gate_ref[0], last, preferred_element_type=f32)
    row_grad += lax.dot_general(value_grad, value_ref[0], last, preferred_element_type=f32)
    row_grad = row_grad.astype(bf16)
    for c in range(total // chunk):
        pieces = []
        for kind in (expert_out, row_grad):
            for s in range(2):
                at = (c * 2 + s) * devices
                for h in range(2):
                    pieces.append(kind[at : at + devices, h * half : (h + 1) * half])
        stacked = jnp.concatenate(pieces, axis=0)
        reply_ref[c * chunk : (c + 1) * chunk, :] = lax.dot_general(
            order, stacked, first, preferred_element_type=f32
        ).astype(bf16)


def combine_body(back_ref, chooser_ref, combined_ref, spread_ref):
    copies, rows, width = spread_ref.shape
    half = width // 2
    summed = jnp.dot(chooser_ref[...], back_ref[...], preferred_element_type=f32)
    for h in range(2):
        lanes = slice(h * half, (h + 1) * half)
        at = 3 * rows * h
        high, low = summed[at : at + rows], summed[at + rows : at + 2 * rows]
        combined_ref[:, lanes] = (high + low).astype(bf16)
        grad = summed[at + 2 * rows : at + 3 * rows].astype(bf16)
        for j in range(copies):
            spread_ref[j, :, lanes] = grad


def backward_body(grad_ref, packed_ref, out_ref, *, scale):
    cores, ny, rows, width = grad_ref.shape
    block = cores * ny * rows
    grads = jnp.concatenate([grad_ref[c, y] for y in range(ny) for c in range(cores)], axis=0)
    out_ref[:, :block] = lax.dot_general(
        packed_ref[:, block:], grads, last, preferred_element_type=f32
    ).astype(bf16)
    weight = jnp.dot(packed_ref[:, :block], grads, preferred_element_type=f32)
    out_ref[:, block:] = (weight * scale).astype(bf16)


def gather_body(parts_ref, weight_ref):
    tiles, tall, half = weight_ref.shape
    block = parts_ref.shape[2] - 2 * half
    total = jnp.sum(parts_ref[:, :, block:].astype(f32), axis=0).astype(bf16)
    for i in range(tiles):
        a, b = i // 2, i % 2
        weight_ref[i] = total[a * tall : (a + 1) * tall, b * half : (b + 1) * half]


def sum_body(parts_ref, out_ref):
    total = jnp.sum(parts_ref[...].astype(f32), axis=0).astype(bf16)
    out_ref[...] = jnp.broadcast_to(total[None], out_ref.shape)


def finish_body(tiles_ref, parts_ref, routed_ref, combined_ref, grad_x_ref, grad_down_ref):
    nx = parts_ref.shape[0]
    block = grad_x_ref.shape[1] // nx
    tiles, tall, half = tiles_ref.shape
    combined_ref[...] = routed_ref[...]
    for j in range(nx):
        grad_x_ref[:, j * block : (j + 1) * block] = parts_ref[j, :, :block]
    for i in range(tiles):
        a, b = i // 2, i % 2
        rows, lanes = slice(a * tall, (a + 1) * tall), slice(b * half, (b + 1) * half)
        grad_down_ref[rows, lanes] = tiles_ref[i].astype(f32)


def on_device(x_t, down_proj, w_gate, w_value, w_out, routes, gate_fix, cotangent):
    nx, ny, nc = lax.axis_size("x"), lax.axis_size("y"), lax.axis_size("c")
    nz = lax.axis_size("dp")
    groups = nx * ny * nc
    feats, width = down_proj.shape
    half = width // 2
    tokens = x_t.shape[1]
    tok_dev = tokens // groups
    block = tokens // nx
    top = routes.shape[1]
    pairs = tok_dev * top
    core = lax.axis_index("c").astype(jnp.int32).reshape(1)

    packed = local(
        pack_body,
        shape(nx, feats, block + width),
        x_t,
        down_proj,
        specs=[hbm, hbm],
        scratch=[
            pltpu.VMEM(x_t.shape, bf16),
            pltpu.VMEM(down_proj.shape, bf16),
            pltpu.SemaphoreType.DMA((2,)),
        ],
        limit=60,
    )
    packed = swap(packed, "x").reshape(nx * feats, block + width)
    mine, theirs = local(
        project_body,
        (shape(ny, tok_dev, width), shape(ny, tok_dev, width)),
        core,
        packed,
        specs=[smem, vmem],
    )
    sent = lax.all_gather(theirs, "c", axis=0, tiled=False)

    flat = routes.reshape(-1)
    chosen = (flat[:, None] == jnp.arange(groups, dtype=jnp.int32)[None, :]).astype(bf16)
    earlier = (jnp.arange(pairs)[:, None] > jnp.arange(pairs)[None, :]).astype(bf16)
    before = jnp.dot(earlier, chosen, preferred_element_type=f32)
    slot_index = jnp.sum(before * chosen.astype(f32), axis=1).astype(jnp.int32)
    target = (flat * 2 + slot_index).reshape(tok_dev, top)

    place = jnp.arange(groups * 8, dtype=jnp.int32)
    slot, kind, part = place // 8 * 2 + place % 4 // 2, place % 8 // 4, place % 2
    hit = slot[:, None, None] == target[None]
    gate_values = gate_fix.astype(f32) / 65536.0
    held = jnp.sum(jnp.where(hit, 1.0, 0.0), axis=2)
    gated = jnp.sum(jnp.where(hit, gate_values[None], 0.0), axis=2)
    where = jnp.concatenate(
        [
            jnp.where((kind == q // 2) & (part == q % 2), 1.0, 0.0)[:, None]
            * (held if q < 2 else gated)
            for q in range(4)
        ],
        axis=1,
    )
    spread = jnp.where(target[:, :, None] == slot[None, None, :], 1.0, 0.0)
    high = jnp.sum(spread * (gate_fix // 256).astype(f32)[:, :, None], axis=1) * (1.0 / 256.0)
    low = jnp.sum(spread * (gate_fix % 256).astype(f32)[:, :, None], axis=1) * (1.0 / 65536.0)
    one = jnp.sum(spread, axis=1)
    chooser = jnp.concatenate(
        [
            jnp.where(((kind == k) & (part == h))[None, :], value, 0.0)
            for h in range(2)
            for k, value in ((0, high), (0, low), (1, one))
        ],
        axis=0,
    ).astype(bf16)

    partial = local(
        add_body,
        shape(ny, tok_dev, width),
        core,
        mine,
        sent,
        where,
        chooser,
        specs=[smem, vmem, vmem, anywhere, anywhere],
    )
    parts = swap(partial, "y")
    send = local(
        dispatch_body,
        shape(groups * 8, half),
        parts,
        cotangent,
        where,
    )
    got = swap(send.reshape(groups, 8, half), ("x", "y", "c")).reshape(groups * 8, half)
    reply = local(
        expert_body,
        shape(groups * 8, half),
        got,
        w_gate,
        w_value,
        w_out,
        specs=[vmem, vmem, hbm, hbm],
        scratch=[
            pltpu.VMEM(w_value.shape, bf16),
            pltpu.VMEM(w_out.shape, bf16),
            pltpu.SemaphoreType.DMA((2, 4)),
        ],
        limit=50,
    )
    back = swap(reply.reshape(groups, 8, half), ("x", "y", "c")).reshape(groups * 8, half)
    routed, by_owner = local(
        combine_body, (shape(tok_dev, width), shape(ny, tok_dev, width)), back, chooser
    )

    by_y = swap(by_owner, "y")
    by_core = lax.all_gather(by_y, "c", axis=0, tiled=False)
    packed_back = local(
        backward_body,
        shape(nx * feats, block + width),
        by_core,
        packed,
        scale=1.0 / math.sqrt(tokens * nz),
    )
    packed_back = swap(packed_back.reshape(nx, feats, block + width), "x")
    weight_tiles = local(gather_body, shape(16, feats // 8, half), packed_back)

    tall = 16 // nz * feats // 8
    own = swap(weight_tiles.reshape(nz, tall, half), "dp")
    own = local(sum_body, shape(nz, tall, half), own)
    tiles = swap(own, "dp").reshape(16, feats // 8, half)
    return local(
        finish_body,
        (shape(tok_dev, width), shape(feats, tokens), shape(feats, width, dtype=f32)),
        tiles,
        packed_back,
        routed,
    )


def solution(mesh):
    dp = mesh.shape["dp"]
    core = 2
    ny = 8
    nx = mesh.shape["expert"] // (ny * core)
    fine = Mesh(mesh.devices.reshape(nx, ny, core, dp), ("x", "y", "c", "dp"))
    expert = ("x", "y", "c")
    tokens = ("dp", "x", "y", "c")
    placed = (
        P(expert, "dp"),
        P(expert, None),
        P(expert, None, None),
        P(expert, None, None),
        P(expert, None, None),
        P(tokens, None),
        P(tokens, None),
        P(tokens, None),
    )
    return jax.shard_map(
        on_device,
        mesh=fine,
        in_specs=placed,
        out_specs=(P(tokens, None), P(expert, "dp"), P(expert, None)),
        check_vma=False,
    )
```

```python
import functools
import math

import jax
import jax.numpy as jnp
from jax import lax
from jax.experimental import pallas as pl
from jax.experimental.pallas import tpu as pltpu
from jax.sharding import Mesh
from jax.sharding import PartitionSpec as P

f32 = jnp.float32
bf16 = jnp.bfloat16
MiB = 1 << 20
last = (((1,), (1,)), ((), ()))
first = (((0,), (0,)), ((), ()))


def swap(blocks, axes):
    return lax.all_to_all(blocks, axes, split_axis=0, concat_axis=0, tiled=True)


vmem = pl.BlockSpec(memory_space=pltpu.VMEM)
smem = pl.BlockSpec(memory_space=pltpu.SMEM)
anywhere = pl.BlockSpec(memory_space=pl.ANY)
hbm = pl.BlockSpec(memory_space=pltpu.HBM)


def local(body, outs, *args, specs=None, out_spec=vmem, scratch=(), limit=8, **static):
    return pl.pallas_call(
        functools.partial(body, **static) if static else body,
        out_shape=outs,
        in_specs=[vmem] * len(args) if specs is None else specs,
        out_specs=jax.tree.map(lambda _: out_spec, outs),
        scratch_shapes=list(scratch),
        compiler_params=pltpu.CompilerParams(vmem_limit_bytes=limit * MiB),
    )(*args)


def shape(*dims, dtype=bf16):
    return jax.ShapeDtypeStruct(dims, dtype)


def pack_body(x_hbm, proj_hbm, out_ref, x_ref, proj_ref, sems):
    pieces, _, wide = out_ref.shape
    block = wide - proj_ref.shape[1]
    loads = [
        pltpu.make_async_copy(x_hbm, x_ref, sems.at[0]),
        pltpu.make_async_copy(proj_hbm, proj_ref, sems.at[1]),
    ]
    for load in loads:
        load.start()
    loads[0].wait()
    for j in range(pieces):
        out_ref[j, :, :block] = x_ref[:, j * block : (j + 1) * block]
    loads[1].wait()
    for j in range(pieces):
        out_ref[j, :, block:] = proj_ref[...]


def project_body(core_ref, packed_ref, mine_ref, theirs_ref):
    ny, rows, width = mine_ref.shape
    block = packed_ref.shape[1] - width
    part = lax.dot_general(
        packed_ref[:, :block], packed_ref[:, block:], first, preferred_element_type=f32
    )
    part = part.astype(bf16).reshape(ny, 2, rows, width)
    even = core_ref[0] == 0
    mine_ref[...] = jnp.where(even, part[:, 0], part[:, 1])
    theirs_ref[...] = jnp.where(even, part[:, 1], part[:, 0])


def add_body(core_ref, mine_ref, sent_ref, _place, _chooser, out_ref):
    other = jnp.where(core_ref[0] == 0, sent_ref[1], sent_ref[0])
    out_ref[...] = (mine_ref[...].astype(f32) + other.astype(f32)).astype(bf16)


def dispatch_body(parts_ref, cot_ref, place_ref, out_ref):
    half = out_ref.shape[1]
    latent = jnp.sum(parts_ref[...].astype(f32), axis=0).astype(bf16)
    cot = cot_ref[...]
    table = jnp.concatenate([latent[:, :half], latent[:, half:], cot[:, :half], cot[:, half:]], 0)
    place = place_ref[...]
    chosen = jnp.where(place != 0.0, 1.0, 0.0).astype(bf16)
    scale = jnp.sum(place, axis=1, keepdims=True)
    rows = jnp.dot(chosen, table, preferred_element_type=f32)
    out_ref[...] = (rows * scale).astype(bf16)


def expert_body(
    got_ref, gate_ref, value_hbm, outw_hbm, reply_ref, value_ref, outw_ref, sems
):
    loads = []
    count = sems.shape[1]
    for i, (source, target) in enumerate(
        ((value_hbm, value_ref), (outw_hbm, outw_ref))
    ):
        tall = source.shape[1] // count
        loads.append(
            [
                pltpu.make_async_copy(
                    source.at[0, pl.ds(j * tall, tall)],
                    target.at[0, pl.ds(j * tall, tall)],
                    sems.at[i, j],
                )
                for j in range(count)
            ]
        )
    for group in loads:
        for load in group:
            load.start()

    def arrived(i):
        for load in loads[i]:
            load.wait()

    total, half = got_ref.shape
    chunk = 256
    devices = chunk // 8
    to = lax.broadcasted_iota(jnp.int32, (chunk, chunk), 0)
    source = lax.broadcasted_iota(jnp.int32, (chunk, chunk), 1)
    order = jnp.where((to % devices) * 8 + to // devices == source, 1.0, 0.0).astype(bf16)
    sorted_rows = [
        jnp.dot(order, got_ref[c * chunk : (c + 1) * chunk, :], preferred_element_type=f32).astype(
            bf16
        )
        for c in range(total // chunk)
    ]

    def matrix(kind):
        halves = []
        for h in range(2):
            pieces = []
            for piece in sorted_rows:
                for s in range(2):
                    r = (kind * 2 + s) * 2 + h
                    pieces.append(piece[r * devices : (r + 1) * devices])
            halves.append(jnp.concatenate(pieces, axis=0))
        return jnp.concatenate(halves, axis=1)

    rows, grads = matrix(0), matrix(1)
    pre_gate = jnp.dot(rows, gate_ref[0], preferred_element_type=f32)
    arrived(0)
    pre_value = jnp.dot(rows, value_ref[0], preferred_element_type=f32)
    arrived(1)
    hidden_grad = lax.dot_general(grads, outw_ref[0], last, preferred_element_type=f32)
    sigmoid_gate = jax.nn.sigmoid(pre_gate)
    activated = pre_gate * sigmoid_gate
    hidden = (activated * pre_value).astype(bf16)
    gate_grad = (
        hidden_grad * pre_value * sigmoid_gate * (1.0 + pre_gate * (1.0 - sigmoid_gate))
    ).astype(bf16)
    value_grad = (hidden_grad * activated).astype(bf16)
    expert_out = jnp.dot(hidden, outw_ref[0], preferred_element_type=f32).astype(bf16)
    row_grad = lax.dot_general(gate_grad, gate_ref[0], last, preferred_element_type=f32)
    row_grad += lax.dot_general(value_grad, value_ref[0], last, preferred_element_type=f32)
    row_grad = row_grad.astype(bf16)
    for c in range(total // chunk):
        pieces = []
        for kind in (expert_out, row_grad):
            for s in range(2):
                at = (c * 2 + s) * devices
                for h in range(2):
                    pieces.append(kind[at : at + devices, h * half : (h + 1) * half])
        stacked = jnp.concatenate(pieces, axis=0)
        reply_ref[c * chunk : (c + 1) * chunk, :] = lax.dot_general(
            order, stacked, first, preferred_element_type=f32
        ).astype(bf16)


def combine_body(back_ref, chooser_ref, combined_ref, spread_ref):
    copies, rows, width = spread_ref.shape
    half = width // 2
    summed = jnp.dot(chooser_ref[...], back_ref[...], preferred_element_type=f32)
    for h in range(2):
        lanes = slice(h * half, (h + 1) * half)
        at = 3 * rows * h
        high, low = summed[at : at + rows], summed[at + rows : at + 2 * rows]
        combined_ref[:, lanes] = (high + low).astype(bf16)
        grad = summed[at + 2 * rows : at + 3 * rows].astype(bf16)
        for j in range(copies):
            spread_ref[j, :, lanes] = grad


def backward_body(grad_ref, packed_ref, out_ref, *, scale):
    cores, ny, rows, width = grad_ref.shape
    block = cores * ny * rows
    grads = jnp.concatenate([grad_ref[c, y] for y in range(ny) for c in range(cores)], axis=0)
    out_ref[:, :block] = lax.dot_general(
        packed_ref[:, block:], grads, last, preferred_element_type=f32
    ).astype(bf16)
    weight = jnp.dot(packed_ref[:, :block], grads, preferred_element_type=f32)
    out_ref[:, block:] = (weight * scale).astype(bf16)


def gather_body(parts_ref, weight_ref):
    tiles, tall, wide = weight_ref.shape
    width = wide * 4
    block = parts_ref.shape[2] - width
    total = jnp.sum(parts_ref[:, :, block:].astype(f32), axis=0).astype(bf16)
    for i in range(tiles):
        a, b = i // 4, i % 4
        weight_ref[i] = total[a * tall : (a + 1) * tall, b * wide : (b + 1) * wide]


def sum_body(parts_ref, out_ref):
    total = jnp.sum(parts_ref[...].astype(f32), axis=0).astype(bf16)
    out_ref[...] = jnp.broadcast_to(total[None], out_ref.shape)


def finish_body(tiles_ref, parts_ref, routed_ref, combined_ref, grad_x_ref, grad_down_ref):
    nx = parts_ref.shape[0]
    block = grad_x_ref.shape[1] // nx
    tiles, tall, wide = tiles_ref.shape
    combined_ref[...] = routed_ref[...]
    for j in range(nx):
        grad_x_ref[:, j * block : (j + 1) * block] = parts_ref[j, :, :block]
    for i in range(tiles):
        a, b = i // 4, i % 4
        rows, lanes = slice(a * tall, (a + 1) * tall), slice(b * wide, (b + 1) * wide)
        grad_down_ref[rows, lanes] = tiles_ref[i].astype(f32)


def on_device(x_t, down_proj, w_gate, w_value, w_out, routes, gate_fix, cotangent):
    nx, ny, nc = lax.axis_size("x"), lax.axis_size("y"), lax.axis_size("c")
    nz = lax.axis_size("dp")
    groups = nx * ny * nc
    feats, width = down_proj.shape
    half = width // 2
    tokens = x_t.shape[1]
    tok_dev = tokens // groups
    block = tokens // nx
    top = routes.shape[1]
    pairs = tok_dev * top
    core = lax.axis_index("c").astype(jnp.int32).reshape(1)

    packed = local(
        pack_body,
        shape(nx, feats, block + width),
        x_t,
        down_proj,
        specs=[hbm, hbm],
        scratch=[
            pltpu.VMEM(x_t.shape, bf16),
            pltpu.VMEM(down_proj.shape, bf16),
            pltpu.SemaphoreType.DMA((2,)),
        ],
        limit=60,
    )
    packed = swap(packed, "x").reshape(nx * feats, block + width)
    mine, theirs = local(
        project_body,
        (shape(ny, tok_dev, width), shape(ny, tok_dev, width)),
        core,
        packed,
        specs=[smem, vmem],
    )
    sent = lax.all_gather(theirs, "c", axis=0, tiled=False)

    flat = routes.reshape(-1)
    chosen = (flat[:, None] == jnp.arange(groups, dtype=jnp.int32)[None, :]).astype(bf16)
    earlier = (jnp.arange(pairs)[:, None] > jnp.arange(pairs)[None, :]).astype(bf16)
    before = jnp.dot(earlier, chosen, preferred_element_type=f32)
    slot_index = jnp.sum(before * chosen.astype(f32), axis=1).astype(jnp.int32)
    target = (flat * 2 + slot_index).reshape(tok_dev, top)

    place = jnp.arange(groups * 8, dtype=jnp.int32)
    slot, kind, part = place // 8 * 2 + place % 4 // 2, place % 8 // 4, place % 2
    hit = slot[:, None, None] == target[None]
    gate_values = gate_fix.astype(f32) / 65536.0
    held = jnp.sum(jnp.where(hit, 1.0, 0.0), axis=2)
    gated = jnp.sum(jnp.where(hit, gate_values[None], 0.0), axis=2)
    where = jnp.concatenate(
        [
            jnp.where((kind == q // 2) & (part == q % 2), 1.0, 0.0)[:, None]
            * (held if q < 2 else gated)
            for q in range(4)
        ],
        axis=1,
    )
    spread = jnp.where(target[:, :, None] == slot[None, None, :], 1.0, 0.0)
    high = jnp.sum(spread * (gate_fix // 256).astype(f32)[:, :, None], axis=1) * (1.0 / 256.0)
    low = jnp.sum(spread * (gate_fix % 256).astype(f32)[:, :, None], axis=1) * (1.0 / 65536.0)
    one = jnp.sum(spread, axis=1)
    chooser = jnp.concatenate(
        [
            jnp.where(((kind == k) & (part == h))[None, :], value, 0.0)
            for h in range(2)
            for k, value in ((0, high), (0, low), (1, one))
        ],
        axis=0,
    ).astype(bf16)

    partial = local(
        add_body,
        shape(ny, tok_dev, width),
        core,
        mine,
        sent,
        where,
        chooser,
        specs=[smem, vmem, vmem, anywhere, anywhere],
    )
    parts = swap(partial, "y")
    send = local(
        dispatch_body,
        shape(groups * 8, half),
        parts,
        cotangent,
        where,
    )
    got = swap(send.reshape(groups, 8, half), ("x", "y", "c")).reshape(groups * 8, half)
    reply = local(
        expert_body,
        shape(groups * 8, half),
        got,
        w_gate,
        w_value,
        w_out,
        specs=[vmem, vmem, hbm, hbm],
        scratch=[
            pltpu.VMEM(w_value.shape, bf16),
            pltpu.VMEM(w_out.shape, bf16),
            pltpu.SemaphoreType.DMA((2, 4)),
        ],
        limit=50,
    )
    back = swap(reply.reshape(groups, 8, half), ("x", "y", "c")).reshape(groups * 8, half)
    routed, by_owner = local(
        combine_body, (shape(tok_dev, width), shape(ny, tok_dev, width)), back, chooser
    )

    by_y = swap(by_owner, "y")
    by_core = lax.all_gather(by_y, "c", axis=0, tiled=False)
    packed_back = local(
        backward_body,
        shape(nx * feats, block + width),
        by_core,
        packed,
        scale=1.0 / math.sqrt(tokens * nz),
    )
    packed_back = swap(packed_back.reshape(nx, feats, block + width), "x")
    weight_tiles = local(gather_body, shape(16, feats // 4, width // 4), packed_back)

    tall = 16 // nz * feats // 4
    own = swap(weight_tiles.reshape(nz, tall, width // 4), "dp")
    own = local(sum_body, shape(nz, tall, width // 4), own)
    tiles = swap(own, "dp").reshape(16, feats // 4, width // 4)
    return local(
        finish_body,
        (shape(tok_dev, width), shape(feats, tokens), shape(feats, width, dtype=f32)),
        tiles,
        packed_back,
        routed,
    )


def solution(mesh):
    dp = mesh.shape["dp"]
    core = 2
    ny = 8
    nx = mesh.shape["expert"] // (ny * core)
    fine = Mesh(mesh.devices.reshape(nx, ny, core, dp), ("x", "y", "c", "dp"))
    expert = ("x", "y", "c")
    tokens = ("dp", "x", "y", "c")
    placed = (
        P(expert, "dp"),
        P(expert, None),
        P(expert, None, None),
        P(expert, None, None),
        P(expert, None, None),
        P(tokens, None),
        P(tokens, None),
        P(tokens, None),
    )
    return jax.shard_map(
        on_device,
        mesh=fine,
        in_specs=placed,
        out_specs=(P(tokens, None), P(expert, "dp"), P(expert, None)),
        check_vma=False,
    )
```

```python
import functools
import math

import jax
import jax.numpy as jnp
from jax import lax
from jax.experimental import pallas as pl
from jax.experimental.pallas import tpu as pltpu
from jax.sharding import Mesh
from jax.sharding import PartitionSpec as P

f32 = jnp.float32
bf16 = jnp.bfloat16
MiB = 1 << 20
last = (((1,), (1,)), ((), ()))
first = (((0,), (0,)), ((), ()))


def swap(blocks, axes):
    return lax.all_to_all(blocks, axes, split_axis=0, concat_axis=0, tiled=True)


vmem = pl.BlockSpec(memory_space=pltpu.VMEM)
smem = pl.BlockSpec(memory_space=pltpu.SMEM)
anywhere = pl.BlockSpec(memory_space=pl.ANY)
hbm = pl.BlockSpec(memory_space=pltpu.HBM)


def local(body, outs, *args, specs=None, out_spec=vmem, scratch=(), limit=8, **static):
    return pl.pallas_call(
        functools.partial(body, **static) if static else body,
        out_shape=outs,
        in_specs=[vmem] * len(args) if specs is None else specs,
        out_specs=jax.tree.map(lambda _: out_spec, outs),
        scratch_shapes=list(scratch),
        compiler_params=pltpu.CompilerParams(vmem_limit_bytes=limit * MiB),
    )(*args)


def shape(*dims, dtype=bf16):
    return jax.ShapeDtypeStruct(dims, dtype)


def pack_body(x_hbm, proj_hbm, out_ref, x_ref, proj_ref, sems):
    pieces, _, wide = out_ref.shape
    block = wide - proj_ref.shape[1]
    loads = [
        pltpu.make_async_copy(x_hbm, x_ref, sems.at[0]),
        pltpu.make_async_copy(proj_hbm, proj_ref, sems.at[1]),
    ]
    for load in loads:
        load.start()
    loads[0].wait()
    for j in range(pieces):
        out_ref[j, :, :block] = x_ref[:, j * block : (j + 1) * block]
    loads[1].wait()
    for j in range(pieces):
        out_ref[j, :, block:] = proj_ref[...]


def project_body(core_ref, packed_ref, mine_ref, theirs_ref):
    ny, rows, width = mine_ref.shape
    block = packed_ref.shape[1] - width
    part = lax.dot_general(
        packed_ref[:, :block], packed_ref[:, block:], first, preferred_element_type=f32
    )
    part = part.astype(bf16).reshape(ny, 2, rows, width)
    even = core_ref[0] == 0
    mine_ref[...] = jnp.where(even, part[:, 0], part[:, 1])
    theirs_ref[...] = jnp.where(even, part[:, 1], part[:, 0])


def add_body(core_ref, mine_ref, sent_ref, _place, _chooser, out_ref):
    other = jnp.where(core_ref[0] == 0, sent_ref[1], sent_ref[0])
    out_ref[...] = (mine_ref[...].astype(f32) + other.astype(f32)).astype(bf16)


def dispatch_body(parts_ref, cot_ref, place_ref, out_ref):
    half = out_ref.shape[1]
    latent = jnp.sum(parts_ref[...].astype(f32), axis=0).astype(bf16)
    cot = cot_ref[...]
    table = jnp.concatenate([latent[:, :half], latent[:, half:], cot[:, :half], cot[:, half:]], 0)
    place = place_ref[...]
    chosen = jnp.where(place != 0.0, 1.0, 0.0).astype(bf16)
    scale = jnp.sum(place, axis=1, keepdims=True)
    rows = jnp.dot(chosen, table, preferred_element_type=f32)
    out_ref[...] = (rows * scale).astype(bf16)


def expert_body(
    got_ref, gate_ref, value_hbm, outw_hbm, reply_ref, value_ref, outw_ref, sems
):
    loads = []
    count = sems.shape[1]
    for i, (source, target) in enumerate(
        ((value_hbm, value_ref), (outw_hbm, outw_ref))
    ):
        tall = source.shape[1] // count
        loads.append(
            [
                pltpu.make_async_copy(
                    source.at[0, pl.ds(j * tall, tall)],
                    target.at[0, pl.ds(j * tall, tall)],
                    sems.at[i, j],
                )
                for j in range(count)
            ]
        )
    for group in loads:
        for load in group:
            load.start()

    def arrived(i):
        for load in loads[i]:
            load.wait()

    total, half = got_ref.shape
    chunk = 256
    devices = chunk // 8
    to = lax.broadcasted_iota(jnp.int32, (chunk, chunk), 0)
    source = lax.broadcasted_iota(jnp.int32, (chunk, chunk), 1)
    order = jnp.where((to % devices) * 8 + to // devices == source, 1.0, 0.0).astype(bf16)
    sorted_rows = [
        jnp.dot(order, got_ref[c * chunk : (c + 1) * chunk, :], preferred_element_type=f32).astype(
            bf16
        )
        for c in range(total // chunk)
    ]

    def matrix(kind):
        halves = []
        for h in range(2):
            pieces = []
            for piece in sorted_rows:
                for s in range(2):
                    r = (kind * 2 + s) * 2 + h
                    pieces.append(piece[r * devices : (r + 1) * devices])
            halves.append(jnp.concatenate(pieces, axis=0))
        return jnp.concatenate(halves, axis=1)

    rows, grads = matrix(0), matrix(1)
    pre_gate = jnp.dot(rows, gate_ref[0], preferred_element_type=f32)
    arrived(0)
    pre_value = jnp.dot(rows, value_ref[0], preferred_element_type=f32)
    arrived(1)
    hidden_grad = lax.dot_general(grads, outw_ref[0], last, preferred_element_type=f32)
    sigmoid_gate = jax.nn.sigmoid(pre_gate)
    activated = pre_gate * sigmoid_gate
    hidden = (activated * pre_value).astype(bf16)
    gate_grad = (
        hidden_grad * pre_value * sigmoid_gate * (1.0 + pre_gate * (1.0 - sigmoid_gate))
    ).astype(bf16)
    value_grad = (hidden_grad * activated).astype(bf16)
    expert_out = jnp.dot(hidden, outw_ref[0], preferred_element_type=f32).astype(bf16)
    row_grad = lax.dot_general(gate_grad, gate_ref[0], last, preferred_element_type=f32)
    row_grad += lax.dot_general(value_grad, value_ref[0], last, preferred_element_type=f32)
    row_grad = row_grad.astype(bf16)
    for c in range(total // chunk):
        pieces = []
        for kind in (expert_out, row_grad):
            for s in range(2):
                at = (c * 2 + s) * devices
                for h in range(2):
                    pieces.append(kind[at : at + devices, h * half : (h + 1) * half])
        stacked = jnp.concatenate(pieces, axis=0)
        reply_ref[c * chunk : (c + 1) * chunk, :] = lax.dot_general(
            order, stacked, first, preferred_element_type=f32
        ).astype(bf16)


def combine_body(back_ref, chooser_ref, combined_ref, spread_ref):
    copies, rows, width = spread_ref.shape
    half = width // 2
    summed = jnp.dot(chooser_ref[...], back_ref[...], preferred_element_type=f32)
    for h in range(2):
        lanes = slice(h * half, (h + 1) * half)
        at = 3 * rows * h
        high, low = summed[at : at + rows], summed[at + rows : at + 2 * rows]
        combined_ref[:, lanes] = (high + low).astype(bf16)
        grad = summed[at + 2 * rows : at + 3 * rows].astype(bf16)
        for j in range(copies):
            spread_ref[j, :, lanes] = grad


def backward_body(grad_ref, packed_ref, out_ref, *, scale):
    cores, ny, rows, width = grad_ref.shape
    block = cores * ny * rows
    grads = jnp.concatenate([grad_ref[c, y] for y in range(ny) for c in range(cores)], axis=0)
    out_ref[:, :block] = lax.dot_general(
        packed_ref[:, block:], grads, last, preferred_element_type=f32
    ).astype(bf16)
    weight = jnp.dot(packed_ref[:, :block], grads, preferred_element_type=f32)
    out_ref[:, block:] = (weight * scale).astype(bf16)


def gather_body(parts_ref, weight_ref):
    tiles, tall, wide = weight_ref.shape
    width = wide * 4
    block = parts_ref.shape[2] - width
    total = jnp.sum(parts_ref[:, :, block:].astype(f32), axis=0).astype(bf16)
    for i in range(tiles):
        a, b = i // 4, i % 4
        weight_ref[i] = total[a * tall : (a + 1) * tall, b * wide : (b + 1) * wide]


def sum_body(parts_ref, out_ref):
    total = jnp.sum(parts_ref[...].astype(f32), axis=0).astype(bf16)
    out_ref[...] = jnp.broadcast_to(total[None], out_ref.shape)


def finish_body(tiles_ref, parts_ref, routed_ref, combined_ref, grad_x_ref, grad_down_ref):
    nx = parts_ref.shape[0]
    block = grad_x_ref.shape[1] // nx
    tiles, tall, wide = tiles_ref.shape
    combined_ref[...] = routed_ref[...]
    for j in range(nx):
        grad_x_ref[:, j * block : (j + 1) * block] = parts_ref[j, :, :block]
    for i in range(tiles):
        a, b = i // 4, i % 4
        rows, lanes = slice(a * tall, (a + 1) * tall), slice(b * wide, (b + 1) * wide)
        grad_down_ref[rows, lanes] = tiles_ref[i].astype(f32)


def on_device(x_t, down_proj, w_gate, w_value, w_out, routes, gate_fix, cotangent):
    nx, ny, nc = lax.axis_size("x"), lax.axis_size("y"), lax.axis_size("c")
    far, near = lax.axis_size("zh"), lax.axis_size("zl")
    nz = far * near
    groups = nx * ny * nc
    feats, width = down_proj.shape
    half = width // 2
    tokens = x_t.shape[1]
    tok_dev = tokens // groups
    block = tokens // nx
    top = routes.shape[1]
    pairs = tok_dev * top
    core = lax.axis_index("c").astype(jnp.int32).reshape(1)

    packed = local(
        pack_body,
        shape(nx, feats, block + width),
        x_t,
        down_proj,
        specs=[hbm, hbm],
        scratch=[
            pltpu.VMEM(x_t.shape, bf16),
            pltpu.VMEM(down_proj.shape, bf16),
            pltpu.SemaphoreType.DMA((2,)),
        ],
        limit=60,
    )
    packed = swap(packed, "x").reshape(nx * feats, block + width)
    mine, theirs = local(
        project_body,
        (shape(ny, tok_dev, width), shape(ny, tok_dev, width)),
        core,
        packed,
        specs=[smem, vmem],
    )
    sent = lax.all_gather(theirs, "c", axis=0, tiled=False)

    flat = routes.reshape(-1)
    chosen = (flat[:, None] == jnp.arange(groups, dtype=jnp.int32)[None, :]).astype(bf16)
    earlier = (jnp.arange(pairs)[:, None] > jnp.arange(pairs)[None, :]).astype(bf16)
    before = jnp.dot(earlier, chosen, preferred_element_type=f32)
    slot_index = jnp.sum(before * chosen.astype(f32), axis=1).astype(jnp.int32)
    target = (flat * 2 + slot_index).reshape(tok_dev, top)

    place = jnp.arange(groups * 8, dtype=jnp.int32)
    slot, kind, part = place // 8 * 2 + place % 4 // 2, place % 8 // 4, place % 2
    hit = slot[:, None, None] == target[None]
    gate_values = gate_fix.astype(f32) / 65536.0
    held = jnp.sum(jnp.where(hit, 1.0, 0.0), axis=2)
    gated = jnp.sum(jnp.where(hit, gate_values[None], 0.0), axis=2)
    where = jnp.concatenate(
        [
            jnp.where((kind == q // 2) & (part == q % 2), 1.0, 0.0)[:, None]
            * (held if q < 2 else gated)
            for q in range(4)
        ],
        axis=1,
    )
    spread = jnp.where(target[:, :, None] == slot[None, None, :], 1.0, 0.0)
    high = jnp.sum(spread * (gate_fix // 256).astype(f32)[:, :, None], axis=1) * (1.0 / 256.0)
    low = jnp.sum(spread * (gate_fix % 256).astype(f32)[:, :, None], axis=1) * (1.0 / 65536.0)
    one = jnp.sum(spread, axis=1)
    chooser = jnp.concatenate(
        [
            jnp.where(((kind == k) & (part == h))[None, :], value, 0.0)
            for h in range(2)
            for k, value in ((0, high), (0, low), (1, one))
        ],
        axis=0,
    ).astype(bf16)

    partial = local(
        add_body,
        shape(ny, tok_dev, width),
        core,
        mine,
        sent,
        where,
        chooser,
        specs=[smem, vmem, vmem, anywhere, anywhere],
    )
    parts = swap(partial, "y")
    send = local(
        dispatch_body,
        shape(groups * 8, half),
        parts,
        cotangent,
        where,
    )
    got = swap(send.reshape(groups, 8, half), ("x", "y", "c")).reshape(groups * 8, half)
    reply = local(
        expert_body,
        shape(groups * 8, half),
        got,
        w_gate,
        w_value,
        w_out,
        specs=[vmem, vmem, hbm, hbm],
        scratch=[
            pltpu.VMEM(w_value.shape, bf16),
            pltpu.VMEM(w_out.shape, bf16),
            pltpu.SemaphoreType.DMA((2, 4)),
        ],
        limit=50,
    )
    back = swap(reply.reshape(groups, 8, half), ("x", "y", "c")).reshape(groups * 8, half)
    routed, by_owner = local(
        combine_body, (shape(tok_dev, width), shape(ny, tok_dev, width)), back, chooser
    )

    by_y = swap(by_owner, "y")
    by_core = lax.all_gather(by_y, "c", axis=0, tiled=False)
    packed_back = local(
        backward_body,
        shape(nx * feats, block + width),
        by_core,
        packed,
        scale=1.0 / math.sqrt(tokens * nz),
    )
    packed_back = swap(packed_back.reshape(nx, feats, block + width), "x")
    weight_tiles = local(gather_body, shape(16, feats // 4, width // 4), packed_back)

    tall = 16 // near * feats // 4
    own = swap(weight_tiles.reshape(near, tall, width // 4), "zl")
    own = local(sum_body, shape(far, tall, width // 4), own)
    own = local(sum_body, shape(near, tall, width // 4), swap(own, "zh"))
    tiles = swap(own, "zl").reshape(16, feats // 4, width // 4)
    return local(
        finish_body,
        (shape(tok_dev, width), shape(feats, tokens), shape(feats, width, dtype=f32)),
        tiles,
        packed_back,
        routed,
    )


def solution(mesh):
    dp = mesh.shape["dp"]
    core = 2
    ny = 8
    nx = mesh.shape["expert"] // (ny * core)
    near = 4
    fine = Mesh(
        mesh.devices.reshape(nx, ny, core, dp // near, near), ("x", "y", "c", "zh", "zl")
    )
    batch = ("zh", "zl")
    expert = ("x", "y", "c")
    tokens = ("zh", "zl", "x", "y", "c")
    placed = (
        P(expert, batch),
        P(expert, None),
        P(expert, None, None),
        P(expert, None, None),
        P(expert, None, None),
        P(tokens, None),
        P(tokens, None),
        P(tokens, None),
    )
    return jax.shard_map(
        on_device,
        mesh=fine,
        in_specs=placed,
        out_specs=(P(tokens, None), P(expert, batch), P(expert, None)),
        check_vma=False,
    )
```
